256 devices in a mesh: row: 16 (over z_hi, y, core), col: 16 (over z_lo, x).
Axes of the slice: x: 4, y: 4, z: 8 (z_hi: 2, z_lo: 4; z = z_hi * 4 + z_lo), core: 2. Of those that a mesh axis runs over, the one named last changes fastest.
Arguments:
- objects: float32 [2, 2, 4096, 4096], P(None, None, 'row', 'col'), may hold values from -5 to 5
- probe: float32 [2, 256, 256], replicated, may hold values from -6 to 6
- prev_partial: float32 [16, 16, 2, 256, 256], P('row', 'col'), may hold values from -6 to 6
- offsets: int32 [16, 16, 1, 2], P('row', 'col'), may hold values from 0 to 128
- counts: int32 [16, 16], P('row', 'col'), may hold values from 0 to 1
- amplitudes: float32 [16, 16, 1, 256, 256], P('row', 'col'), may hold values from 1 to 2.5
Outputs:
- new_objects: float32 [2, 2, 4096, 4096], P(None, None, 'row', 'col')
- new_probe: float32 [2, 256, 256], replicated
- new_partial: float32 [16, 16, 2, 256, 256], P('row', 'col')
The draws below stay inside these ranges and needn't reach their ends.
All inputs are finite; a program needn't handle non-finite values.
Results may differ from the reference program's by a relative error of at most 0.0003.
Values sent between devices are 32-bit elements; how exact they have to be, the bound alone decides.
No kernel may reach another device: no remote copies, remote signals or barrier semaphores. Data moves between devices by JAX's collectives and lax.ppermute only.
A program may use at most 64 MiB of HBM per device.

```python
import math
import jax
import jax.numpy as jnp
from jax import lax

WIN = 256
HALO = 64
TILE = 256
PAT = 1
NY = 4096
NX = 4096
N_ROW = 16
N_COL = 16


def with_ends(drawn, stream_key, low, top_value):
    shape = drawn.shape
    place = [jax.random.randint(jax.random.fold_in(stream_key, axis), (), 0, shape[axis]) for axis in range(len(shape))]
    drawn = drawn.at[tuple(place)].set(low)
    longest = shape.index(max(shape))
    place[longest] = (place[longest] + 1) % shape[longest]
    return drawn.at[tuple(place)].set(top_value)


def shard_levels(stream_key, shape, shards, least, high):
    def one(dim, parts):
        draws = jax.random.uniform(jax.random.fold_in(jax.random.fold_in(stream_key, 6), dim), (parts,), jnp.float32, least / len(shards), high / len(shards))
        return jnp.repeat(jnp.exp(draws), shape[dim] // parts).reshape((-1,) + (1,) * (len(shape) - dim - 1))

    level = one(*shards[0])
    for cut in shards[1:]:
        level = level * one(*cut)
    return level


def gaussian(own_key, shape, scale, limit, pieces=(), held_as=jnp.bfloat16):
    array = scale * jax.random.normal(own_key, shape, jnp.float32)
    if pieces:
        array = array * shard_levels(own_key, shape, pieces, -0.22, 0.18)
    return jnp.clip(array, -limit, limit).astype(held_as)


def setup_inputs(seed: int = 0) -> dict:
    key_of = jax.random.split(jax.random.key(seed), 7)
    return {
        "objects": gaussian(key_of[0], (2, 2, NY, NX), 0.7, 5.0, ((2, 16), (3, 16)), jnp.float32),
        "probe": gaussian(key_of[1], (2, WIN, WIN), 1.0, 6.0, (), jnp.float32),
        "prev_partial": gaussian(key_of[2], (N_ROW, N_COL, 2, WIN, WIN), 1.0, 6.0, ((0, 16), (1, 16)), jnp.float32),
        "offsets": with_ends(jax.random.randint(key_of[3], (N_ROW, N_COL, PAT, 2), 0, TILE + 2 * HALO - WIN + 1), jax.random.fold_in(key_of[3], 1), 0, TILE + 2 * HALO - WIN).astype(jnp.int32),
        "counts": with_ends(jax.random.randint(key_of[4], (N_ROW, N_COL), 0, PAT + 1), jax.random.fold_in(key_of[4], 1), 0, PAT).astype(jnp.int32),
        "amplitudes": jnp.clip(1.0 + 1.5 * jax.random.uniform(key_of[5], (N_ROW, N_COL, PAT, WIN, WIN), jnp.float32) ** shard_levels(key_of[5], (N_ROW, N_COL, PAT, WIN, WIN), ((0, 16), (1, 16)), -0.2, 0.2), 1.0, 2.5),
    }


OBJ_RATE = 0.1
PROBE_RATE = 0.3

def fresnel(n):
    index = jnp.arange(n, dtype=jnp.int32)
    freq = jnp.where(index < n // 2, index, index - n)
    square = (freq * freq).astype(jnp.float32)
    phase = jnp.pi * (square[:, None] + square[None, :]) / (4.0 * n)
    return (jnp.cos(phase), jnp.sin(phase))

def pattern_loss(ext, probe, offset, live, amp):
    zero = jnp.zeros((), jnp.int32)
    window = lax.dynamic_slice(ext, (zero, zero, offset[0].astype(jnp.int32), offset[1].astype(jnp.int32)), (2, 2, WIN, WIN))
    first = lax.complex(window[0, 0], window[0, 1])
    second = lax.complex(window[1, 0], window[1, 1])
    wave = lax.complex(probe[0], probe[1]) * first
    hre, him = fresnel(WIN)
    spectrum = jnp.fft.fft2(wave, norm='ortho') * lax.complex(hre, him)
    wave = jnp.fft.ifft2(spectrum, norm='ortho') * second
    far = jnp.fft.fft2(wave, norm='ortho')
    power = jnp.real(far) ** 2 + jnp.imag(far) ** 2
    return live * jnp.sum((jnp.sqrt(power + 1.0) - amp) ** 2)

def local_grads(ext, probe, offsets, count, amps):
    live = (jnp.arange(PAT, dtype=jnp.int32) < count).astype(jnp.float32)

    def total(ext_in, probe_in):
        losses = jax.vmap(pattern_loss, in_axes=(None, None, 0, 0, 0))(ext_in, probe_in, offsets, live, amps)
        return jnp.sum(losses)
    return jax.grad(total, argnums=(0, 1))(ext, probe)

def reference(objects, probe, prev_partial, offsets, counts, amplitudes):
    padded = jnp.pad(objects, ((0, 0), (0, 0), (HALO, HALO), (HALO, HALO)))
    side = TILE + 2 * HALO
    zero = jnp.zeros((), jnp.int32)

    def visit(grad_pad, index):
        tile_row = index // N_COL
        tile_col = index % N_COL
        top = (tile_row * TILE).astype(jnp.int32)
        left = (tile_col * TILE).astype(jnp.int32)
        ext = lax.dynamic_slice(padded, (zero, zero, top, left), (2, 2, side, side))
        grad_ext, grad_probe = local_grads(ext, probe, offsets[tile_row, tile_col], counts[tile_row, tile_col], amplitudes[tile_row, tile_col])
        old = lax.dynamic_slice(grad_pad, (zero, zero, top, left), (2, 2, side, side))
        grad_pad = lax.dynamic_update_slice(grad_pad, old + grad_ext, (zero, zero, top, left))
        return (grad_pad, grad_probe)
    start = jnp.zeros(padded.shape, jnp.float32)
    grad_pad, partials = lax.scan(visit, start, jnp.arange(N_ROW * N_COL, dtype=jnp.int32))
    grad = grad_pad[:, :, HALO:HALO + NY, HALO:HALO + NX]
    new_partial = partials.reshape(N_ROW, N_COL, 2, WIN, WIN)
    total = lax.optimization_barrier(jnp.sum(prev_partial, axis=(0, 1)))
    rate = PROBE_RATE / math.sqrt(N_ROW * N_COL)
    return (objects - OBJ_RATE * grad, probe - rate * total, new_partial)
```

```python
import math

import jax
import jax.numpy as jnp
import ml_dtypes
import numpy as np
from jax import lax
from jax.experimental import pallas as pl
from jax.experimental.pallas import tpu as pltpu
from jax.sharding import Mesh
from jax.sharding import PartitionSpec as P

WIN = 256
HALO = 64
TILE = 256
SIDE = TILE + 2 * HALO
AXES = ("row_0", "row_1", "row_2", "col_0", "col_1")
ROW = ("row_0", "row_1", "row_2")
COL = ("col_0", "col_1")
PLANE = ("row_1", "col_1", "row_2")
DEPTH = ("row_0", "col_0")

OBJ_RATE = 0.1
PROBE_RATE = 0.3
VMEM = pl.BlockSpec(memory_space=pltpu.VMEM)
SMEM = pl.BlockSpec(memory_space=pltpu.SMEM)
PARAMS = pltpu.CompilerParams(vmem_limit_bytes=48 * 1024 * 1024)


def operator_parts():
    index = np.arange(WIN)
    angle = 2.0 * np.pi * (index[:, None] * index[None, :] % WIN) / WIN
    forward = np.exp(-1j * angle) / math.sqrt(WIN)
    freq = np.where(index < WIN // 2, index, index - WIN)
    shift = np.exp(1j * np.pi * freq.astype(np.float64) ** 2 / (4.0 * WIN))
    propagate = np.conj(forward) @ (shift[:, None] * forward)
    parts = []
    for matrix in (propagate, forward):
        matrix = (matrix + matrix.T) / 2
        halves = []
        for part in (matrix.real, matrix.imag, -matrix.imag):
            high = part.astype(np.float32).astype(ml_dtypes.bfloat16)
            low = (part - high.astype(np.float64)).astype(np.float32)
            halves.append((high, low.astype(ml_dtypes.bfloat16)))
        parts += [high for high, _ in halves] + [low for _, low in halves]
    return np.stack(parts)


def halves_of(value):
    high = value.astype(jnp.bfloat16)
    low = (value - high.astype(jnp.float32)).astype(jnp.bfloat16)
    return high, low


def dot(left, right):
    return jnp.dot(left, right, preferred_element_type=jnp.float32)


def three(left, right):
    (left_high, left_low), (right_high, right_low) = left, right
    return dot(left_high, right_high) + (dot(left_low, right_high) + dot(left_high, right_low))


def sandwich(mats, which, real_part, imag_part):
    def block(rows):
        return jnp.concatenate(
            [jnp.concatenate([mats[6 * which + k] for k in row], axis=1) for row in rows], axis=0
        )

    right = tuple(block(((3 * h, 3 * h + 1), (3 * h + 2, 3 * h))) for h in range(2))
    left = tuple(block(((3 * h, 3 * h + 2), (3 * h + 1, 3 * h))) for h in range(2))
    inner = three(halves_of(jnp.concatenate([real_part, imag_part], axis=1)), right)
    stacked = jnp.concatenate([inner[:, :WIN], inner[:, WIN:]], axis=0)
    outer = three(left, halves_of(stacked))
    return outer[:WIN], outer[WIN:]


def first_half(shape):
    return lax.broadcasted_iota(jnp.int32, shape, len(shape) - 1) < HALO


def pack_columns(objects, north, south, west_send, east_send):
    for s in range(2):
        for src, start, size in ((north, 0, HALO), (objects, HALO, TILE), (south, HALO + TILE, HALO)):
            rows = pl.ds(start, size)
            real, imag = src[s, 0], src[s, 1]
            keep = first_half((size, 2 * HALO))
            west_send[s, rows] = jnp.where(keep, real[:, :128], pltpu.roll(imag[:, :128], HALO, 1))
            east_send[s, rows] = jnp.where(keep, pltpu.roll(real[:, 128:], HALO, 1), imag[:, 128:])


def gradient(
    offset, count, objects, north, south, west, east, probe, amp, mats,
    center, north_out, south_out, west_out, east_out, probe_out, ext, grad,
):
    keep = first_half((SIDE, 2 * HALO))
    for s in range(2):
        for k in range(2):
            ext[2 * s + k, :HALO, :TILE] = north[s, k]
            ext[2 * s + k, HALO : HALO + TILE, :TILE] = objects[s, k]
            ext[2 * s + k, HALO + TILE : SIDE, :TILE] = south[s, k]
        ext[2 * s, :SIDE, TILE:] = jnp.where(keep, east[s], pltpu.roll(west[s], HALO, 1))
        ext[2 * s + 1, :SIDE, TILE:] = jnp.where(keep, pltpu.roll(east[s], HALO, 1), west[s])
    grad[...] = jnp.zeros_like(grad)
    top, left = offset[0], offset[1]
    into = lax.rem(SIDE + HALO - left, SIDE)
    back = lax.rem(SIDE - HALO + left, SIDE)

    low = lax.rem(top, 8)
    rows = pl.ds(pl.multiple_of(top - low, 8), WIN + 8)

    def window(k):
        wide = pltpu.roll(ext[k, rows, :], into, 1)[:, :WIN]
        return pltpu.roll(wide, lax.rem(WIN + 8 - low, WIN + 8), 0)[:WIN]

    def place(k, value):
        tall = jnp.concatenate([value, jnp.zeros((8, WIN), jnp.float32)], axis=0)
        tall = pltpu.roll(tall, low, 0)
        wide = jnp.concatenate([tall, jnp.zeros((WIN + 8, SIDE - WIN), jnp.float32)], axis=1)
        grad[k, rows, :] = pltpu.roll(wide, back, 1)

    a_re, a_im, b_re, b_im = (window(k) for k in range(4))
    p_re, p_im = probe[0], probe[1]
    u_re = p_re * a_re - p_im * a_im
    u_im = p_re * a_im + p_im * a_re
    v_re, v_im = sandwich(mats, 0, u_re, u_im)
    e_re = v_re * b_re - v_im * b_im
    e_im = v_re * b_im + v_im * b_re
    w_re, w_im = sandwich(mats, 1, e_re, e_im)
    size = jnp.sqrt(w_re * w_re + w_im * w_im + 1.0)
    live = jnp.where(count[0] > 0, 2.0, 0.0)
    slope = live * (size - amp[...]) / size
    e_re, e_im = sandwich(mats, 1, slope * w_re, -slope * w_im)
    place(2, -OBJ_RATE * (e_re * v_re - e_im * v_im))
    place(3, OBJ_RATE * (e_re * v_im + e_im * v_re))
    v_re = e_re * b_re - e_im * b_im
    v_im = e_re * b_im + e_im * b_re
    u_re, u_im = sandwich(mats, 0, v_re, v_im)
    place(0, -OBJ_RATE * (u_re * p_re - u_im * p_im))
    place(1, OBJ_RATE * (u_re * p_im + u_im * p_re))
    probe_out[0] = u_re * a_re - u_im * a_im
    probe_out[1] = -(u_re * a_im + u_im * a_re)
    for s in range(2):
        for k in range(2):
            north_out[s, k] = grad[2 * s + k, :HALO, :TILE]
            south_out[s, k] = grad[2 * s + k, HALO + TILE : SIDE, :TILE]
            center[s, k] = objects[s, k] + grad[2 * s + k, HALO : HALO + TILE, :TILE]
        real, imag = grad[2 * s, :SIDE, TILE:], grad[2 * s + 1, :SIDE, TILE:]
        east_out[s] = jnp.where(keep, real, pltpu.roll(imag, HALO, 1))
        west_out[s] = jnp.where(keep, pltpu.roll(real, HALO, 1), imag)


def edge_columns(west, east, s, start, size):
    keep = first_half((size, 2 * HALO))
    w, e = west[s, pl.ds(start, size)], east[s, pl.ds(start, size)]
    zero = jnp.zeros_like(w)
    wr, er = pltpu.roll(w, HALO, 1), pltpu.roll(e, HALO, 1)
    return (
        (jnp.where(keep, w, zero), jnp.where(keep, zero, er)),
        (jnp.where(keep, wr, zero), jnp.where(keep, zero, e)),
    )


def add_margins(north, south, west, east, north_send, south_send):
    for s in range(2):
        for src, dst, start in ((north, north_send, 0), (south, south_send, HALO + TILE)):
            for k, (first, last) in enumerate(edge_columns(west, east, s, start, HALO)):
                dst[s, k, :, :128] = src[s, k, :, :128] + first
                dst[s, k, :, 128:] = src[s, k, :, 128:] + last


def finish(center, west, east, north, south, new_objects):
    for s in range(2):
        for k, (first, last) in enumerate(edge_columns(west, east, s, HALO, TILE)):
            for cols, edge in ((slice(0, 128), first), (slice(128, 256), last)):
                value = center[s, k, :, cols] + edge
                new_objects[s, k, :HALO, cols] = value[:HALO] + north[s, k, :, cols]
                new_objects[s, k, HALO : TILE - HALO, cols] = value[HALO : TILE - HALO]
                new_objects[s, k, TILE - HALO :, cols] = value[TILE - HALO :] + south[s, k, :, cols]


def call(body, outs, *args, specs=None, scratch=(), flops=0, name=None):
    moved = sum(math.prod(o) * 4 for o in outs)
    return pl.pallas_call(
        body,
        out_shape=[jax.ShapeDtypeStruct(o, jnp.float32) for o in outs],
        in_specs=specs or [VMEM] * len(args),
        out_specs=[VMEM] * len(outs),
        scratch_shapes=scratch,
        compiler_params=PARAMS,
        cost_estimate=pl.CostEstimate(flops=flops, bytes_accessed=2 * moved, transcendentals=0),
        name=name,
    )(*args)


def shifted(value, axis, by):
    peers = lax.axis_size(axis)
    return lax.ppermute(value, axis, [(i, i + by) for i in range(peers) if 0 <= i + by < peers])


def swap(value, axes):
    return lax.all_to_all(value, axes, 0, 0, tiled=True)


def probe_sum(partial):
    plane, depth = lax.axis_size(PLANE), lax.axis_size(DEPTH)
    rows = 2 * WIN // plane
    part = jnp.sum(swap(partial.reshape(plane, rows, WIN), PLANE), axis=0)
    part = jnp.sum(swap(jnp.broadcast_to(part, (depth, rows, WIN)), DEPTH), axis=0)
    return swap(jnp.broadcast_to(part, (plane, rows, WIN)), PLANE).reshape(2, WIN, WIN)


def shards(objects, probe, prev_partial, offsets, counts, amplitudes):
    strip, column = (2, 2, HALO, TILE), (2, SIDE, 2 * HALO)
    tile = (2, 2, TILE, TILE)
    north = shifted(objects[:, :, TILE - HALO :, :], ROW, 1)
    south = shifted(objects[:, :, :HALO, :], ROW, -1)
    west_send, east_send = call(pack_columns, [column] * 2, objects, north, south, name="pack")
    west = shifted(east_send, COL, 1)
    east = shifted(west_send, COL, -1)
    center, north_part, south_part, west_part, east_part, partial = call(
        gradient,
        [tile, strip, strip, column, column, (2, WIN, WIN)],
        offsets.reshape(2), counts.reshape(1), objects, north, south, west, east, probe,
        amplitudes.reshape(WIN, WIN), jnp.asarray(operator_parts()),
        specs=[SMEM, SMEM] + [VMEM] * 8,
        scratch=[pltpu.VMEM((4, SIDE + 8, SIDE), jnp.float32)] * 2,
        flops=96 * 2 * WIN**3,
        name="gradient",
    )
    from_west = shifted(east_part, COL, 1)
    from_east = shifted(west_part, COL, -1)
    north_send, south_send = call(
        add_margins, [strip] * 2, north_part, south_part, from_west, from_east, name="margins"
    )
    from_north = shifted(south_send, ROW, 1)
    from_south = shifted(north_send, ROW, -1)
    (new_objects,) = call(
        finish, [tile], center, from_west, from_east, from_north, from_south, name="finish"
    )
    rate = PROBE_RATE / math.sqrt(lax.axis_size(ROW) * lax.axis_size(COL))
    new_probe = probe - rate * probe_sum(prev_partial)
    return (new_objects, new_probe, partial[None, None])


def solution(mesh):
    split = Mesh(mesh.devices.reshape(2, 4, 2, 4, 4), AXES)
    return jax.shard_map(
        shards,
        mesh=split,
        in_specs=(
            P(None, None, ROW, COL),
            P(),
            P(ROW, COL, None, None, None),
            P(ROW, COL, None, None),
            P(ROW, COL),
            P(ROW, COL, None, None, None),
        ),
        out_specs=(P(None, None, ROW, COL), P(), P(ROW, COL, None, None, None)),
        check_vma=False,
    )
```

```python
import math

import jax
import jax.numpy as jnp
import ml_dtypes
import numpy as np
from jax import lax
from jax.experimental import pallas as pl
from jax.experimental.pallas import tpu as pltpu
from jax.sharding import Mesh
from jax.sharding import PartitionSpec as P

WIN = 256
HALO = 64
TILE = 256
SIDE = TILE + 2 * HALO
AXES = ("row_0", "row_1", "row_2", "col_0", "col_1")
ROW = ("row_0", "row_1", "row_2")
COL = ("col_0", "col_1")
PLANE = ("row_1", "col_1")
PAIR = "row_2"
DEPTH = ("row_0", "col_0")

OBJ_RATE = 0.1
PROBE_RATE = 0.3
VMEM = pl.BlockSpec(memory_space=pltpu.VMEM)
HBM = pl.BlockSpec(memory_space=pltpu.HBM)
ANY = pl.BlockSpec(memory_space=pl.ANY)
SMEM = pl.BlockSpec(memory_space=pltpu.SMEM)
MIB = 1024 * 1024


def operator_parts():
    index = np.arange(WIN)
    angle = 2.0 * np.pi * (index[:, None] * index[None, :] % WIN) / WIN
    forward = np.exp(-1j * angle) / math.sqrt(WIN)
    freq = np.where(index < WIN // 2, index, index - WIN)
    shift = np.exp(1j * np.pi * freq.astype(np.float64) ** 2 / (4.0 * WIN))
    propagate = np.conj(forward) @ (shift[:, None] * forward)
    parts = []
    for matrix in (propagate, forward):
        matrix = (matrix + matrix.T) / 2
        halves = []
        for part in (matrix.real, matrix.imag, -matrix.imag):
            high = part.astype(np.float32).astype(ml_dtypes.bfloat16)
            low = (part - high.astype(np.float64)).astype(np.float32)
            halves.append((high, low.astype(ml_dtypes.bfloat16)))
        parts += [high for high, _ in halves] + [low for _, low in halves]
    return np.stack(parts)


def halves_of(value):
    high = value.astype(jnp.bfloat16)
    low = (value - high.astype(jnp.float32)).astype(jnp.bfloat16)
    return high, low


def dot(left, right):
    return jnp.dot(left, right, preferred_element_type=jnp.float32)


def three(left, right):
    (left_high, left_low), (right_high, right_low) = left, right
    return dot(left_high, right_high) + (dot(left_low, right_high) + dot(left_high, right_low))


def sandwich(mats, which, real_part, imag_part):
    def block(rows):
        return jnp.concatenate(
            [jnp.concatenate([mats[6 * which + k] for k in row], axis=1) for row in rows], axis=0
        )

    right = tuple(block(((3 * h, 3 * h + 1), (3 * h + 2, 3 * h))) for h in range(2))
    left = tuple(block(((3 * h, 3 * h + 2), (3 * h + 1, 3 * h))) for h in range(2))
    inner = three(halves_of(jnp.concatenate([real_part, imag_part], axis=1)), right)
    stacked = jnp.concatenate([inner[:, :WIN], inner[:, WIN:]], axis=0)
    outer = three(left, halves_of(stacked))
    return outer[:WIN], outer[WIN:]


def first_half(shape):
    return lax.broadcasted_iota(jnp.int32, shape, len(shape) - 1) < HALO


def side_columns(src, s, size):
    real, imag = src[s, 0], src[s, 1]
    keep = first_half((size, 2 * HALO))
    return (
        jnp.where(keep, real[:, :128], pltpu.roll(imag[:, :128], HALO, 1)),
        jnp.where(keep, pltpu.roll(real[:, 128:], HALO, 1), imag[:, 128:]),
    )


def either(flag, when_even, when_odd):
    return jnp.where(flag == 0, when_even, when_odd)


def pack_sides(facts, objects, row_a, row_b, col_a, col_b):
    row_odd, col_odd = facts[3], facts[4]
    for s in range(2):
        top, bottom = objects[s, :, :HALO], objects[s, :, TILE - HALO :]
        row_a[s] = either(row_odd, bottom, top)
        row_b[s] = either(row_odd, top, bottom)
        first, last = side_columns(objects, s, TILE)
        col_a[s] = either(col_odd, last, first)
        col_b[s] = either(col_odd, first, last)


def pack_corners(facts, row_a, row_b, col_a, col_b):
    row_odd, col_odd = facts[3], facts[4]
    for s in range(2):
        a, b = side_columns(row_a, s, HALO), side_columns(row_b, s, HALO)
        for rows, when_even, when_odd in ((pl.ds(0, HALO), b, a), (pl.ds(HALO, HALO), a, b)):
            first, last = (either(row_odd, *pair) for pair in zip(when_even, when_odd))
            col_a[s, rows] = either(col_odd, last, first)
            col_b[s, rows] = either(col_odd, first, last)


def gradient(
    facts, objects, row_a, row_b, col_a, col_b, corners_a, corners_b, probe, amp, mats,
    center_out, north_out, south_out, col_a_out, col_b_out, corners_a_out, corners_b_out, probe_out,
    ext, grad, sides, sides_out, probe_in, amp_in, mats_in, probe_grad, arrive, leave,
):
    row_odd, col_odd = facts[3], facts[4]
    across = pl.ds(0, TILE)
    middle, upper, lower = pl.ds(HALO, TILE), pl.ds(0, HALO), pl.ds(HALO + TILE, HALO)

    def beyond(odd):
        return pl.ds(pl.multiple_of((1 - odd) * (HALO + TILE), HALO), HALO)

    incoming = [
        (objects, ext.at[:, :, middle, across]),
        (row_a, ext.at[:, :, beyond(row_odd), across]),
        (row_b, ext.at[:, :, beyond(1 - row_odd), across]),
        (probe, probe_in),
        (mats, mats_in),
        (amp, amp_in),
    ]
    outgoing = [(probe_grad, probe_out)]
    for side, col, corner, col_out, corner_out in (
        (1 - col_odd, col_a, corners_a, col_a_out, corners_a_out),
        (col_odd, col_b, corners_b, col_b_out, corners_b_out),
    ):
        for rows, src, dst in (
            (upper, corner.at[:, upper], corner_out.at[:, upper]),
            (middle, col, col_out),
            (lower, corner.at[:, pl.ds(HALO, HALO)], corner_out.at[:, pl.ds(HALO, HALO)]),
        ):
            incoming.insert(3, (src, sides.at[side, :, rows]))
            outgoing.append((sides_out.at[side, :, rows], dst))
    outgoing += [
        (grad.at[:, :, upper, across], north_out),
        (grad.at[:, :, lower, across], south_out),
        (ext.at[:, :, middle, across], center_out),
    ]
    coming = [pltpu.make_async_copy(*pair, arrive.at[i]) for i, pair in enumerate(incoming)]
    going = [pltpu.make_async_copy(*pair, leave.at[i]) for i, pair in enumerate(outgoing)]
    for copy in coming:
        copy.start()
    grad[...] = jnp.zeros_like(grad)
    for copy in coming[:-3]:
        copy.wait()
    keep = first_half((SIDE, 2 * HALO))
    for s in range(2):
        w, e = sides[0, s], sides[1, s]
        ext[s, 0, :SIDE, TILE:] = jnp.where(keep, e, pltpu.roll(w, HALO, 1))
        ext[s, 1, :SIDE, TILE:] = jnp.where(keep, pltpu.roll(e, HALO, 1), w)
    top, left = facts[0], facts[1]
    into = lax.rem(SIDE + HALO - left, SIDE)
    back = lax.rem(SIDE - HALO + left, SIDE)
    low = lax.rem(top, 8)
    rows = pl.ds(pl.multiple_of(top - low, 8), WIN + 8)

    def window(s, k):
        wide = pltpu.roll(ext[s, k, rows, :], into, 1)[:, :WIN]
        return pltpu.roll(wide, lax.rem(WIN + 8 - low, WIN + 8), 0)[:WIN]

    def place(s, k, value):
        tall = jnp.concatenate([value, jnp.zeros((8, WIN), jnp.float32)], axis=0)
        tall = pltpu.roll(tall, low, 0)
        wide = jnp.concatenate([tall, jnp.zeros((WIN + 8, SIDE - WIN), jnp.float32)], axis=1)
        grad[s, k, rows, :] = pltpu.roll(wide, back, 1)

    a_re, a_im, b_re, b_im = window(0, 0), window(0, 1), window(1, 0), window(1, 1)
    coming[-3].wait()
    p_re, p_im = probe_in[0], probe_in[1]
    u_re = p_re * a_re - p_im * a_im
    u_im = p_re * a_im + p_im * a_re
    coming[-2].wait()
    v_re, v_im = sandwich(mats_in, 0, u_re, u_im)
    e_re = v_re * b_re - v_im * b_im
    e_im = v_re * b_im + v_im * b_re
    w_re, w_im = sandwich(mats_in, 1, e_re, e_im)
    coming[-1].wait()
    size = jnp.sqrt(w_re * w_re + w_im * w_im + 1.0)
    live = jnp.where(facts[2] > 0, 2.0, 0.0)
    slope = live * (size - amp_in[...]) / size
    e_re, e_im = sandwich(mats_in, 1, slope * w_re, -slope * w_im)
    place(1, 0, -OBJ_RATE * (e_re * v_re - e_im * v_im))
    place(1, 1, OBJ_RATE * (e_re * v_im + e_im * v_re))
    v_re = e_re * b_re - e_im * b_im
    v_im = e_re * b_im + e_im * b_re
    u_re, u_im = sandwich(mats_in, 0, v_re, v_im)
    place(0, 0, -OBJ_RATE * (u_re * p_re - u_im * p_im))
    place(0, 1, OBJ_RATE * (u_re * p_im + u_im * p_re))
    probe_grad[0] = u_re * a_re - u_im * a_im
    probe_grad[1] = -(u_re * a_im + u_im * a_re)
    for s in range(2):
        real, imag = grad[s, 0, :SIDE, TILE:], grad[s, 1, :SIDE, TILE:]
        sides_out[0, s] = jnp.where(keep, pltpu.roll(real, HALO, 1), imag)
        sides_out[1, s] = jnp.where(keep, real, pltpu.roll(imag, HALO, 1))
    for copy in going[:-1]:
        copy.start()
    for s in range(2):
        for k in range(2):
            ext[s, k, middle, :TILE] = ext[s, k, middle, :TILE] + grad[s, k, middle, :TILE]
    going[-1].start()
    for copy in going:
        copy.wait()


def edge_columns(col_odd, col_a, col_b, s, start, size):
    keep = first_half((size, 2 * HALO))
    a, b = col_a[s, pl.ds(start, size)], col_b[s, pl.ds(start, size)]
    w, e = either(col_odd, b, a), either(col_odd, a, b)
    zero = jnp.zeros_like(w)
    wr, er = pltpu.roll(w, HALO, 1), pltpu.roll(e, HALO, 1)
    return (
        (jnp.where(keep, w, zero), jnp.where(keep, zero, er)),
        (jnp.where(keep, wr, zero), jnp.where(keep, zero, e)),
    )


def add_margins(facts, north, south, corners_a, corners_b, row_a, row_b):
    row_odd, col_odd = facts[3], facts[4]
    for s in range(2):
        upper = edge_columns(col_odd, corners_a, corners_b, s, 0, HALO)
        lower = edge_columns(col_odd, corners_a, corners_b, s, HALO, HALO)
        for k in range(2):
            for half, cols in enumerate((slice(0, 128), slice(128, 256))):
                up = north[s, k, :, cols] + upper[k][half]
                down = south[s, k, :, cols] + lower[k][half]
                row_a[s, k, :, cols] = either(row_odd, down, up)
                row_b[s, k, :, cols] = either(row_odd, up, down)


def finish(facts, center, col_a, col_b, row_a, row_b, new_objects):
    row_odd, col_odd = facts[3], facts[4]
    for s in range(2):
        for k, edges in enumerate(edge_columns(col_odd, col_a, col_b, s, 0, TILE)):
            for cols, edge in zip((slice(0, 128), slice(128, 256)), edges):
                value = center[s, k, :, cols] + edge
                a, b = row_a[s, k, :, cols], row_b[s, k, :, cols]
                new_objects[s, k, :HALO, cols] = value[:HALO] + either(row_odd, b, a)
                new_objects[s, k, HALO : TILE - HALO, cols] = value[HALO : TILE - HALO]
                new_objects[s, k, TILE - HALO :, cols] = value[TILE - HALO :] + either(row_odd, a, b)


def call(body, outs, *args, specs=None, scratch=(), flops=0, limit=2, name=None):
    moved = sum(math.prod(o) * 4 for o in outs)
    return pl.pallas_call(
        body,
        out_shape=[jax.ShapeDtypeStruct(o, jnp.float32) for o in outs],
        in_specs=[SMEM] + (specs or [VMEM] * (len(args) - 1)),
        out_specs=[HBM if specs else VMEM] * len(outs),
        scratch_shapes=scratch,
        compiler_params=pltpu.CompilerParams(vmem_limit_bytes=limit * MIB),
        cost_estimate=pl.CostEstimate(flops=flops, bytes_accessed=2 * moved, transcendentals=0),
        name=name,
    )(*args)


def exchanged(value, axis, first):
    pairs = [(i, i + 1) for i in range(first, lax.axis_size(axis) - 1, 2)]
    return lax.ppermute(value, axis, pairs + [(j, i) for i, j in pairs])


def swap(value, axes):
    return lax.all_to_all(value, axes, 0, 0, tiled=True)


def after(value, *others):
    return lax.optimization_barrier((value, *others))[0]


def probe_sum(partial, *marks):
    plane, depth = lax.axis_size(PLANE), lax.axis_size(DEPTH)
    rows = WIN // plane
    core = lax.axis_index(PAIR)
    own, other = (lax.dynamic_index_in_dim(partial, k, 0, False) for k in (core, 1 - core))
    part = own + exchanged(after(other, marks[0]), PAIR, 0)
    part = swap(after(part, marks[1]).reshape(plane, rows, WIN), PLANE)
    part = jnp.sum(after(part, marks[2]), axis=0)
    part = swap(jnp.broadcast_to(part, (depth, rows, WIN)), DEPTH)
    part = jnp.sum(after(part, marks[3]), axis=0)
    own = swap(jnp.broadcast_to(part, (plane, rows, WIN)), PLANE).reshape(WIN, WIN)
    other = exchanged(own, PAIR, 0)
    return jnp.stack([either(core, own, other), either(core, other, own)])


def shards(objects, probe, prev_partial, offsets, counts, amplitudes):
    strip, column, corners = (2, 2, HALO, TILE), (2, TILE, 2 * HALO), (2, 2 * HALO, 2 * HALO)
    tile = (2, 2, TILE, TILE)
    facts = jnp.concatenate([
        offsets.reshape(2), counts.reshape(1),
        jnp.stack([lax.axis_index("row_2"), lax.axis_index("col_1") % 2]).astype(jnp.int32),
    ])
    row_a, row_b, col_a, col_b = call(pack_sides, [strip] * 2 + [column] * 2, facts, objects, name="pack_sides")
    row_b, row_a = exchanged(row_b, ROW, 1), exchanged(row_a, ROW, 0)
    col_b, col_a = exchanged(col_b, COL, 1), exchanged(col_a, COL, 0)
    side_mark = row_a
    sent_a, sent_b = call(pack_corners, [corners] * 2, facts, row_a, row_b, name="pack_corners")
    corners_b, corners_a = exchanged(sent_b, COL, 1), exchanged(sent_a, COL, 0)
    center, north, south, col_a_part, col_b_part, corners_a_part, corners_b_part, partial = call(
        gradient,
        [tile, strip, strip, column, column, corners, corners, (2, WIN, WIN)],
        facts, objects, row_a, row_b, col_a, col_b, corners_a, corners_b, probe,
        amplitudes.reshape(WIN, WIN), jnp.asarray(operator_parts()),
        specs=[ANY] * 3 + [HBM] * 7,
        scratch=[pltpu.VMEM((2, 2, SIDE + 8, SIDE), jnp.float32)] * 2
        + [pltpu.VMEM((2, 2, SIDE, 2 * HALO), jnp.float32)] * 2
        + [pltpu.VMEM((2, WIN, WIN), jnp.float32), pltpu.VMEM((WIN, WIN), jnp.float32)]
        + [pltpu.VMEM((12, WIN, WIN), jnp.bfloat16), pltpu.VMEM((2, WIN, WIN), jnp.float32)]
        + [pltpu.SemaphoreType.DMA((12,)), pltpu.SemaphoreType.DMA((10,))],
        flops=96 * 2 * WIN**3,
        limit=60,
        name="gradient",
    )
    corners_b, corners_a = exchanged(corners_b_part, COL, 1), exchanged(corners_a_part, COL, 0)
    corners_a, corners_b, col_a_part, col_b_part = lax.optimization_barrier(
        (corners_a, corners_b, col_a_part, col_b_part)
    )
    row_a, row_b = call(add_margins, [strip] * 2, facts, north, south, corners_a, corners_b, name="margins")
    row_b, row_a = exchanged(row_b, ROW, 1), exchanged(row_a, ROW, 0)
    col_b, col_a = exchanged(col_b_part, COL, 1), exchanged(col_a_part, COL, 0)
    (new_objects,) = call(finish, [tile], facts, center, col_a, col_b, row_a, row_b, name="finish")
    rate = PROBE_RATE / math.sqrt(lax.axis_size(ROW) * lax.axis_size(COL))
    total = probe_sum(prev_partial[0, 0], side_mark, side_mark, partial, corners_a)
    new_probe = probe - rate * total
    return (new_objects, new_probe, partial[None, None])


def solution(mesh):
    split = Mesh(mesh.devices.reshape(2, 4, 2, 4, 4), AXES)
    return jax.shard_map(
        shards,
        mesh=split,
        in_specs=(
            P(None, None, ROW, COL),
            P(),
            P(ROW, COL, None, None, None),
            P(ROW, COL, None, None),
            P(ROW, COL),
            P(ROW, COL, None, None, None),
        ),
        out_specs=(P(None, None, ROW, COL), P(), P(ROW, COL, None, None, None)),
        check_vma=False,
    )
```

```python
import math

import jax
import jax.numpy as jnp
import ml_dtypes
import numpy as np
from jax import lax
from jax.experimental import pallas as pl
from jax.experimental.pallas import tpu as pltpu
from jax.sharding import Mesh
from jax.sharding import PartitionSpec as P

WIN = 256
HALO = 64
TILE = 256
SIDE = TILE + 2 * HALO
AXES = ("row_0", "row_1", "row_2", "col_0", "col_1")
ROW = ("row_0", "row_1", "row_2")
COL = ("col_0", "col_1")
PLANE = ("row_1", "col_1")
PAIR = "row_2"
DEPTH = ("row_0", "col_0")

OBJ_RATE = 0.1
PROBE_RATE = 0.3
VMEM = pl.BlockSpec(memory_space=pltpu.VMEM)
HBM = pl.BlockSpec(memory_space=pltpu.HBM)
ANY = pl.BlockSpec(memory_space=pl.ANY)
SMEM = pl.BlockSpec(memory_space=pltpu.SMEM)
MIB = 1024 * 1024


def operator_parts():
    index = np.arange(WIN)
    angle = 2.0 * np.pi * (index[:, None] * index[None, :] % WIN) / WIN
    forward = np.exp(-1j * angle) / math.sqrt(WIN)
    freq = np.where(index < WIN // 2, index, index - WIN)
    shift = np.exp(1j * np.pi * freq.astype(np.float64) ** 2 / (4.0 * WIN))
    propagate = np.conj(forward) @ (shift[:, None] * forward)
    parts = []
    for matrix in (propagate, forward):
        matrix = (matrix + matrix.T) / 2
        halves = []
        for part in (matrix.real, matrix.imag, -matrix.imag):
            high = part.astype(np.float32).astype(ml_dtypes.bfloat16)
            low = (part - high.astype(np.float64)).astype(np.float32)
            halves.append((high, low.astype(ml_dtypes.bfloat16)))
        parts += [high for high, _ in halves] + [low for _, low in halves]
    return np.stack(parts)


def halves_of(value):
    high = value.astype(jnp.bfloat16)
    low = (value - high.astype(jnp.float32)).astype(jnp.bfloat16)
    return high, low


def dot(left, right):
    return jnp.dot(left, right, preferred_element_type=jnp.float32)


def three(left, right):
    (left_high, left_low), (right_high, right_low) = left, right
    return dot(left_high, right_high) + (dot(left_low, right_high) + dot(left_high, right_low))


def sandwich(mats, which, real_part, imag_part):
    def block(rows):
        return jnp.concatenate(
            [jnp.concatenate([mats[6 * which + k] for k in row], axis=1) for row in rows], axis=0
        )

    right = tuple(block(((3 * h, 3 * h + 1), (3 * h + 2, 3 * h))) for h in range(2))
    left = tuple(block(((3 * h, 3 * h + 2), (3 * h + 1, 3 * h))) for h in range(2))
    inner = three(halves_of(jnp.concatenate([real_part, imag_part], axis=1)), right)
    stacked = jnp.concatenate([inner[:, :WIN], inner[:, WIN:]], axis=0)
    outer = three(left, halves_of(stacked))
    return outer[:WIN], outer[WIN:]


def first_half(shape):
    return lax.broadcasted_iota(jnp.int32, shape, len(shape) - 1) < HALO


def side_columns(src, s, size):
    real, imag = src[s, 0], src[s, 1]
    keep = first_half((size, 2 * HALO))
    return (
        jnp.where(keep, real[:, :128], pltpu.roll(imag[:, :128], HALO, 1)),
        jnp.where(keep, pltpu.roll(real[:, 128:], HALO, 1), imag[:, 128:]),
    )


def either(flag, when_even, when_odd):
    return jnp.where(flag == 0, when_even, when_odd)


def pack_sides(facts, objects, row_a, row_b, col_a, col_b):
    row_odd, col_odd = facts[3], facts[4]
    for s in range(2):
        top, bottom = objects[s, :, :HALO], objects[s, :, TILE - HALO :]
        row_a[s] = either(row_odd, bottom, top)
        row_b[s] = either(row_odd, top, bottom)
        first, last = side_columns(objects, s, TILE)
        col_a[s] = either(col_odd, last, first)
        col_b[s] = either(col_odd, first, last)


def pack_corners(facts, row_a, row_b, col_a, col_b):
    row_odd, col_odd = facts[3], facts[4]
    for s in range(2):
        a, b = side_columns(row_a, s, HALO), side_columns(row_b, s, HALO)
        for rows, when_even, when_odd in ((pl.ds(0, HALO), b, a), (pl.ds(HALO, HALO), a, b)):
            first, last = (either(row_odd, *pair) for pair in zip(when_even, when_odd))
            col_a[s, rows] = either(col_odd, last, first)
            col_b[s, rows] = either(col_odd, first, last)


def gradient(
    facts, objects, row_a, row_b, col_a, col_b, corners_a, corners_b, probe, amp, mats,
    center_out, north_out, south_out, col_a_out, col_b_out, corners_a_out, corners_b_out, probe_out,
    ext, grad, sides, sides_out, probe_in, amp_in, mats_in, probe_grad, arrive, leave,
):
    row_odd, col_odd = facts[3], facts[4]
    across = pl.ds(0, TILE)
    middle, upper, lower = pl.ds(HALO, TILE), pl.ds(0, HALO), pl.ds(HALO + TILE, HALO)

    def beyond(odd):
        return pl.ds(pl.multiple_of((1 - odd) * (HALO + TILE), HALO), HALO)

    incoming = [
        (objects, ext.at[:, :, middle, across]),
        (row_a, ext.at[:, :, beyond(row_odd), across]),
        (row_b, ext.at[:, :, beyond(1 - row_odd), across]),
        (probe, probe_in),
        (mats, mats_in),
        (amp, amp_in),
    ]
    outgoing = [(probe_grad, probe_out)]
    for side, col, corner, col_out, corner_out in (
        (1 - col_odd, col_a, corners_a, col_a_out, corners_a_out),
        (col_odd, col_b, corners_b, col_b_out, corners_b_out),
    ):
        for rows, src, dst in (
            (upper, corner.at[:, upper], corner_out.at[:, upper]),
            (middle, col, col_out),
            (lower, corner.at[:, pl.ds(HALO, HALO)], corner_out.at[:, pl.ds(HALO, HALO)]),
        ):
            incoming.insert(3, (src, sides.at[side, :, rows]))
            outgoing.append((sides_out.at[side, :, rows], dst))
    outgoing += [
        (grad.at[:, :, upper, across], north_out),
        (grad.at[:, :, lower, across], south_out),
        (ext.at[:, :, middle, across], center_out),
    ]
    coming = [pltpu.make_async_copy(*pair, arrive.at[i]) for i, pair in enumerate(incoming)]
    going = [pltpu.make_async_copy(*pair, leave.at[i]) for i, pair in enumerate(outgoing)]
    for copy in coming:
        copy.start()
    grad[...] = jnp.zeros_like(grad)
    for copy in coming[:-3]:
        copy.wait()
    keep = first_half((SIDE, 2 * HALO))
    for s in range(2):
        w, e = sides[0, s], sides[1, s]
        ext[s, 0, :SIDE, TILE:] = jnp.where(keep, e, pltpu.roll(w, HALO, 1))
        ext[s, 1, :SIDE, TILE:] = jnp.where(keep, pltpu.roll(e, HALO, 1), w)
    top, left = facts[0], facts[1]
    into = lax.rem(SIDE + HALO - left, SIDE)
    back = lax.rem(SIDE - HALO + left, SIDE)
    low = lax.rem(top, 8)
    rows = pl.ds(pl.multiple_of(top - low, 8), WIN + 8)

    def window(s, k):
        wide = pltpu.roll(ext[s, k, rows, :], into, 1)[:, :WIN]
        return pltpu.roll(wide, lax.rem(WIN + 8 - low, WIN + 8), 0)[:WIN]

    def place(s, k, value):
        tall = jnp.concatenate([value, jnp.zeros((8, WIN), jnp.float32)], axis=0)
        tall = pltpu.roll(tall, low, 0)
        wide = jnp.concatenate([tall, jnp.zeros((WIN + 8, SIDE - WIN), jnp.float32)], axis=1)
        grad[s, k, rows, :] = pltpu.roll(wide, back, 1)

    a_re, a_im, b_re, b_im = window(0, 0), window(0, 1), window(1, 0), window(1, 1)
    coming[-3].wait()
    p_re, p_im = probe_in[0], probe_in[1]
    u_re = p_re * a_re - p_im * a_im
    u_im = p_re * a_im + p_im * a_re
    coming[-2].wait()
    v_re, v_im = sandwich(mats_in, 0, u_re, u_im)
    e_re = v_re * b_re - v_im * b_im
    e_im = v_re * b_im + v_im * b_re
    w_re, w_im = sandwich(mats_in, 1, e_re, e_im)
    coming[-1].wait()
    size = jnp.sqrt(w_re * w_re + w_im * w_im + 1.0)
    live = jnp.where(facts[2] > 0, 2.0, 0.0)
    slope = live * (size - amp_in[...]) / size
    e_re, e_im = sandwich(mats_in, 1, slope * w_re, -slope * w_im)
    place(1, 0, -OBJ_RATE * (e_re * v_re - e_im * v_im))
    place(1, 1, OBJ_RATE * (e_re * v_im + e_im * v_re))
    v_re = e_re * b_re - e_im * b_im
    v_im = e_re * b_im + e_im * b_re
    u_re, u_im = sandwich(mats_in, 0, v_re, v_im)
    place(0, 0, -OBJ_RATE * (u_re * p_re - u_im * p_im))
    place(0, 1, OBJ_RATE * (u_re * p_im + u_im * p_re))
    probe_grad[0] = u_re * a_re - u_im * a_im
    probe_grad[1] = -(u_re * a_im + u_im * a_re)
    for s in range(2):
        real, imag = grad[s, 0, :SIDE, TILE:], grad[s, 1, :SIDE, TILE:]
        sides_out[0, s] = jnp.where(keep, pltpu.roll(real, HALO, 1), imag)
        sides_out[1, s] = jnp.where(keep, real, pltpu.roll(imag, HALO, 1))
    for copy in going[:-1]:
        copy.start()
    for s in range(2):
        for k in range(2):
            ext[s, k, middle, :TILE] = ext[s, k, middle, :TILE] + grad[s, k, middle, :TILE]
    going[-1].start()
    for copy in going:
        copy.wait()


def edge_columns(col_odd, col_a, col_b, s, start, size):
    keep = first_half((size, 2 * HALO))
    a, b = col_a[s, pl.ds(start, size)], col_b[s, pl.ds(start, size)]
    w, e = either(col_odd, b, a), either(col_odd, a, b)
    zero = jnp.zeros_like(w)
    wr, er = pltpu.roll(w, HALO, 1), pltpu.roll(e, HALO, 1)
    return (
        (jnp.where(keep, w, zero), jnp.where(keep, zero, er)),
        (jnp.where(keep, wr, zero), jnp.where(keep, zero, e)),
    )


def add_margins(facts, north, south, corners_a, corners_b, row_a, row_b):
    row_odd, col_odd = facts[3], facts[4]
    for s in range(2):
        upper = edge_columns(col_odd, corners_a, corners_b, s, 0, HALO)
        lower = edge_columns(col_odd, corners_a, corners_b, s, HALO, HALO)
        for k in range(2):
            for half, cols in enumerate((slice(0, 128), slice(128, 256))):
                up = north[s, k, :, cols] + upper[k][half]
                down = south[s, k, :, cols] + lower[k][half]
                row_a[s, k, :, cols] = either(row_odd, down, up)
                row_b[s, k, :, cols] = either(row_odd, up, down)


def finish(facts, center, col_a, col_b, row_a, row_b, new_objects):
    row_odd, col_odd = facts[3], facts[4]
    for s in range(2):
        for k, edges in enumerate(edge_columns(col_odd, col_a, col_b, s, 0, TILE)):
            for cols, edge in zip((slice(0, 128), slice(128, 256)), edges):
                value = center[s, k, :, cols] + edge
                a, b = row_a[s, k, :, cols], row_b[s, k, :, cols]
                new_objects[s, k, :HALO, cols] = value[:HALO] + either(row_odd, b, a)
                new_objects[s, k, HALO : TILE - HALO, cols] = value[HALO : TILE - HALO]
                new_objects[s, k, TILE - HALO :, cols] = value[TILE - HALO :] + either(row_odd, a, b)


def call(body, outs, *args, specs=None, scratch=(), flops=0, limit=2, name=None):
    moved = sum(math.prod(o) * 4 for o in outs)
    return pl.pallas_call(
        body,
        out_shape=[jax.ShapeDtypeStruct(o, jnp.float32) for o in outs],
        in_specs=[SMEM] + (specs or [VMEM] * (len(args) - 1)),
        out_specs=[HBM if specs else VMEM] * len(outs),
        scratch_shapes=scratch,
        compiler_params=pltpu.CompilerParams(vmem_limit_bytes=limit * MIB),
        cost_estimate=pl.CostEstimate(flops=flops, bytes_accessed=2 * moved, transcendentals=0),
        name=name,
    )(*args)


def exchanged(value, axis, first):
    pairs = [(i, i + 1) for i in range(first, lax.axis_size(axis) - 1, 2)]
    return lax.ppermute(value, axis, pairs + [(j, i) for i, j in pairs])


def swap(value, axes):
    return lax.all_to_all(value, axes, 0, 0, tiled=True)


def after(value, *others):
    return lax.optimization_barrier((value, *others))[0]


def scatter_sum(partial, mark):
    plane = lax.axis_size(PLANE)
    core = lax.axis_index(PAIR)
    own, other = (lax.dynamic_index_in_dim(partial, k, 0, False) for k in (core, 1 - core))
    part = own + exchanged(after(other, mark), PAIR, 0)
    return swap(part.reshape(plane, WIN // plane, WIN), PLANE)


def depth_sum(parts, mark):
    part = jnp.sum(after(parts, mark), axis=0)
    return swap(jnp.broadcast_to(part, (lax.axis_size(DEPTH),) + part.shape), DEPTH)


def gather_sum(parts, mark, last):
    part = jnp.sum(after(parts, mark), axis=0)
    core = lax.axis_index(PAIR)
    own = swap(jnp.broadcast_to(part, (lax.axis_size(PLANE),) + part.shape), PLANE).reshape(WIN, WIN)
    own = after(own, last)
    other = exchanged(own, PAIR, 0)
    return jnp.stack([either(core, own, other), either(core, other, own)])


def shards(objects, probe, prev_partial, offsets, counts, amplitudes):
    strip, column, corners = (2, 2, HALO, TILE), (2, TILE, 2 * HALO), (2, 2 * HALO, 2 * HALO)
    tile = (2, 2, TILE, TILE)
    facts = jnp.concatenate([
        offsets.reshape(2), counts.reshape(1),
        jnp.stack([lax.axis_index("row_2"), lax.axis_index("col_1") % 2]).astype(jnp.int32),
    ])
    row_a, row_b, col_a, col_b = call(pack_sides, [strip] * 2 + [column] * 2, facts, objects, name="pack_sides")
    row_b, row_a = exchanged(row_b, ROW, 1), exchanged(row_a, ROW, 0)
    col_b, col_a = exchanged(col_b, COL, 1), exchanged(col_a, COL, 0)
    scattered = scatter_sum(prev_partial[0, 0], row_a)
    sent_a, sent_b = call(pack_corners, [corners] * 2, facts, row_a, row_b, name="pack_corners")
    corners_b, corners_a = exchanged(sent_b, COL, 1), exchanged(sent_a, COL, 0)
    corners_a, scattered = lax.optimization_barrier((corners_a, scattered))
    center, north, south, col_a_part, col_b_part, corners_a_part, corners_b_part, partial = call(
        gradient,
        [tile, strip, strip, column, column, corners, corners, (2, WIN, WIN)],
        facts, objects, row_a, row_b, col_a, col_b, corners_a, corners_b, probe,
        amplitudes.reshape(WIN, WIN), jnp.asarray(operator_parts()),
        specs=[ANY] * 3 + [HBM] * 7,
        scratch=[pltpu.VMEM((2, 2, SIDE + 8, SIDE), jnp.float32)] * 2
        + [pltpu.VMEM((2, 2, SIDE, 2 * HALO), jnp.float32)] * 2
        + [pltpu.VMEM((2, WIN, WIN), jnp.float32), pltpu.VMEM((WIN, WIN), jnp.float32)]
        + [pltpu.VMEM((12, WIN, WIN), jnp.bfloat16), pltpu.VMEM((2, WIN, WIN), jnp.float32)]
        + [pltpu.SemaphoreType.DMA((12,)), pltpu.SemaphoreType.DMA((10,))],
        flops=96 * 2 * WIN**3,
        limit=60,
        name="gradient",
    )
    corners_b, corners_a = exchanged(corners_b_part, COL, 1), exchanged(corners_a_part, COL, 0)
    deep = depth_sum(scattered, partial)
    corners_a, corners_b, col_a_part, col_b_part, deep = lax.optimization_barrier(
        (corners_a, corners_b, col_a_part, col_b_part, deep)
    )
    row_a, row_b = call(add_margins, [strip] * 2, facts, north, south, corners_a, corners_b, name="margins")
    row_b, row_a = exchanged(row_b, ROW, 1), exchanged(row_a, ROW, 0)
    col_b, col_a = exchanged(col_b_part, COL, 1), exchanged(col_a_part, COL, 0)
    (new_objects,) = call(finish, [tile], facts, center, col_a, col_b, row_a, row_b, flops=10**10, name="finish")
    rate = PROBE_RATE / math.sqrt(lax.axis_size(ROW) * lax.axis_size(COL))
    total = gather_sum(deep, row_a, row_b)
    new_probe = probe - rate * total
    return (new_objects, new_probe, partial[None, None])


def solution(mesh):
    split = Mesh(mesh.devices.reshape(2, 4, 2, 4, 4), AXES)
    return jax.shard_map(
        shards,
        mesh=split,
        in_specs=(
            P(None, None, ROW, COL),
            P(),
            P(ROW, COL, None, None, None),
            P(ROW, COL, None, None),
            P(ROW, COL),
            P(ROW, COL, None, None, None),
        ),
        out_specs=(P(None, None, ROW, COL), P(), P(ROW, COL, None, None, None)),
        check_vma=False,
    )
```

```python
import math

import jax
import jax.numpy as jnp
import ml_dtypes
import numpy as np
from jax import lax
from jax.experimental import pallas as pl
from jax.experimental.pallas import tpu as pltpu
from jax.sharding import Mesh
from jax.sharding import PartitionSpec as P

WIN = 256
HALO = 64
TILE = 256
SIDE = TILE + 2 * HALO
AXES = ("row_0", "row_1", "row_2", "col_0", "col_1")
ROW = ("row_0", "row_1", "row_2")
COL = ("col_0", "col_1")
PLANE = ("row_1", "col_1")
PAIR = "row_2"
DEPTH = ("row_0", "col_0")

OBJ_RATE = 0.1
PROBE_RATE = 0.3
VMEM = pl.BlockSpec(memory_space=pltpu.VMEM)
HBM = pl.BlockSpec(memory_space=pltpu.HBM)
ANY = pl.BlockSpec(memory_space=pl.ANY)
SMEM = pl.BlockSpec(memory_space=pltpu.SMEM)
MIB = 1024 * 1024


def operator_parts():
    index = np.arange(WIN)
    angle = 2.0 * np.pi * (index[:, None] * index[None, :] % WIN) / WIN
    forward = np.exp(-1j * angle) / math.sqrt(WIN)
    freq = np.where(index < WIN // 2, index, index - WIN)
    shift = np.exp(1j * np.pi * freq.astype(np.float64) ** 2 / (4.0 * WIN))
    propagate = np.conj(forward) @ (shift[:, None] * forward)
    parts = []
    for matrix in (propagate, forward):
        matrix = (matrix + matrix.T) / 2
        halves = []
        for part in (matrix.real, matrix.imag, -matrix.imag):
            high = part.astype(np.float32).astype(ml_dtypes.bfloat16)
            low = (part - high.astype(np.float64)).astype(np.float32)
            halves.append((high, low.astype(ml_dtypes.bfloat16)))
        parts += [high for high, _ in halves] + [low for _, low in halves]
    return np.stack(parts)


def halves_of(value):
    high = value.astype(jnp.bfloat16)
    low = (value - high.astype(jnp.float32)).astype(jnp.bfloat16)
    return high, low


def dot(left, right):
    return jnp.dot(left, right, preferred_element_type=jnp.float32)


def three(left, right):
    (left_high, left_low), (right_high, right_low) = left, right
    return dot(left_high, right_high) + (dot(left_low, right_high) + dot(left_high, right_low))


def sandwich(mats, which, real_part, imag_part):
    def block(rows):
        return jnp.concatenate(
            [jnp.concatenate([mats[6 * which + k] for k in row], axis=1) for row in rows], axis=0
        )

    right = tuple(block(((3 * h, 3 * h + 1), (3 * h + 2, 3 * h))) for h in range(2))
    left = tuple(block(((3 * h, 3 * h + 2), (3 * h + 1, 3 * h))) for h in range(2))
    inner = three(halves_of(jnp.concatenate([real_part, imag_part], axis=1)), right)
    stacked = jnp.concatenate([inner[:, :WIN], inner[:, WIN:]], axis=0)
    outer = three(left, halves_of(stacked))
    return outer[:WIN], outer[WIN:]


def first_half(shape):
    return lax.broadcasted_iota(jnp.int32, shape, len(shape) - 1) < HALO


def side_columns(src, s, size):
    real, imag = src[s, 0], src[s, 1]
    keep = first_half((size, 2 * HALO))
    return (
        jnp.where(keep, real[:, :128], pltpu.roll(imag[:, :128], HALO, 1)),
        jnp.where(keep, pltpu.roll(real[:, 128:], HALO, 1), imag[:, 128:]),
    )


def either(flag, when_even, when_odd):
    return jnp.where(flag == 0, when_even, when_odd)


def pack_sides(facts, objects, row_a, row_b, col_a, col_b):
    row_odd, col_odd = facts[3], facts[4]
    for s in range(2):
        top, bottom = objects[s, :, :HALO], objects[s, :, TILE - HALO :]
        row_a[s] = either(row_odd, bottom, top)
        row_b[s] = either(row_odd, top, bottom)
        first, last = side_columns(objects, s, TILE)
        col_a[s] = either(col_odd, last, first)
        col_b[s] = either(col_odd, first, last)


def pack_corners(facts, row_a, row_b, col_a, col_b):
    row_odd, col_odd = facts[3], facts[4]
    for s in range(2):
        a, b = side_columns(row_a, s, HALO), side_columns(row_b, s, HALO)
        for rows, when_even, when_odd in ((pl.ds(0, HALO), b, a), (pl.ds(HALO, HALO), a, b)):
            first, last = (either(row_odd, *pair) for pair in zip(when_even, when_odd))
            col_a[s, rows] = either(col_odd, last, first)
            col_b[s, rows] = either(col_odd, first, last)


def gradient(
    facts, objects, row_a, row_b, col_a, col_b, corners_a, corners_b, probe, amp, mats,
    center_out, north_out, south_out, col_a_out, col_b_out, corners_a_out, corners_b_out, probe_out,
    ext, grad, sides, sides_out, probe_in, amp_in, mats_in, probe_grad, arrive, leave,
):
    row_odd, col_odd = facts[3], facts[4]
    across = pl.ds(0, TILE)
    middle, upper, lower = pl.ds(HALO, TILE), pl.ds(0, HALO), pl.ds(HALO + TILE, HALO)

    def beyond(odd):
        return pl.ds(pl.multiple_of((1 - odd) * (HALO + TILE), HALO), HALO)

    incoming = [
        (objects, ext.at[:, :, middle, across]),
        (row_a, ext.at[:, :, beyond(row_odd), across]),
        (row_b, ext.at[:, :, beyond(1 - row_odd), across]),
        (probe, probe_in),
        (mats, mats_in),
        (amp, amp_in),
    ]
    outgoing = [(probe_grad, probe_out)]
    for side, col, corner, col_out, corner_out in (
        (1 - col_odd, col_a, corners_a, col_a_out, corners_a_out),
        (col_odd, col_b, corners_b, col_b_out, corners_b_out),
    ):
        for rows, src, dst in (
            (upper, corner.at[:, upper], corner_out.at[:, upper]),
            (middle, col, col_out),
            (lower, corner.at[:, pl.ds(HALO, HALO)], corner_out.at[:, pl.ds(HALO, HALO)]),
        ):
            incoming.insert(3, (src, sides.at[side, :, rows]))
            outgoing.append((sides_out.at[side, :, rows], dst))
    outgoing += [
        (grad.at[:, :, upper, across], north_out),
        (grad.at[:, :, lower, across], south_out),
        (ext.at[:, :, middle, across], center_out),
    ]
    coming = [pltpu.make_async_copy(*pair, arrive.at[i]) for i, pair in enumerate(incoming)]
    going = [pltpu.make_async_copy(*pair, leave.at[i]) for i, pair in enumerate(outgoing)]
    for copy in coming:
        copy.start()
    grad[...] = jnp.zeros_like(grad)
    for copy in coming[:-3]:
        copy.wait()
    keep = first_half((SIDE, 2 * HALO))
    for s in range(2):
        w, e = sides[0, s], sides[1, s]
        ext[s, 0, :SIDE, TILE:] = jnp.where(keep, e, pltpu.roll(w, HALO, 1))
        ext[s, 1, :SIDE, TILE:] = jnp.where(keep, pltpu.roll(e, HALO, 1), w)
    top, left = facts[0], facts[1]
    into = lax.rem(SIDE + HALO - left, SIDE)
    back = lax.rem(SIDE - HALO + left, SIDE)
    low = lax.rem(top, 8)
    rows = pl.ds(pl.multiple_of(top - low, 8), WIN + 8)

    def window(s, k):
        wide = pltpu.roll(ext[s, k, rows, :], into, 1)[:, :WIN]
        return pltpu.roll(wide, lax.rem(WIN + 8 - low, WIN + 8), 0)[:WIN]

    def place(s, k, value):
        tall = jnp.concatenate([value, jnp.zeros((8, WIN), jnp.float32)], axis=0)
        tall = pltpu.roll(tall, low, 0)
        wide = jnp.concatenate([tall, jnp.zeros((WIN + 8, SIDE - WIN), jnp.float32)], axis=1)
        grad[s, k, rows, :] = pltpu.roll(wide, back, 1)

    a_re, a_im, b_re, b_im = window(0, 0), window(0, 1), window(1, 0), window(1, 1)
    coming[-3].wait()
    p_re, p_im = probe_in[0], probe_in[1]
    u_re = p_re * a_re - p_im * a_im
    u_im = p_re * a_im + p_im * a_re
    coming[-2].wait()
    v_re, v_im = sandwich(mats_in, 0, u_re, u_im)
    e_re = v_re * b_re - v_im * b_im
    e_im = v_re * b_im + v_im * b_re
    w_re, w_im = sandwich(mats_in, 1, e_re, e_im)
    coming[-1].wait()
    size = jnp.sqrt(w_re * w_re + w_im * w_im + 1.0)
    live = jnp.where(facts[2] > 0, 2.0, 0.0)
    slope = live * (size - amp_in[...]) / size
    e_re, e_im = sandwich(mats_in, 1, slope * w_re, -slope * w_im)
    place(1, 0, -OBJ_RATE * (e_re * v_re - e_im * v_im))
    place(1, 1, OBJ_RATE * (e_re * v_im + e_im * v_re))
    v_re = e_re * b_re - e_im * b_im
    v_im = e_re * b_im + e_im * b_re
    u_re, u_im = sandwich(mats_in, 0, v_re, v_im)
    place(0, 0, -OBJ_RATE * (u_re * p_re - u_im * p_im))
    place(0, 1, OBJ_RATE * (u_re * p_im + u_im * p_re))
    probe_grad[0] = u_re * a_re - u_im * a_im
    probe_grad[1] = -(u_re * a_im + u_im * a_re)
    for s in range(2):
        real, imag = grad[s, 0, :SIDE, TILE:], grad[s, 1, :SIDE, TILE:]
        sides_out[0, s] = jnp.where(keep, pltpu.roll(real, HALO, 1), imag)
        sides_out[1, s] = jnp.where(keep, real, pltpu.roll(imag, HALO, 1))
    for copy in going[:-1]:
        copy.start()
    for s in range(2):
        for k in range(2):
            ext[s, k, middle, :TILE] = ext[s, k, middle, :TILE] + grad[s, k, middle, :TILE]
    going[-1].start()
    for copy in going:
        copy.wait()


def edge_columns(col_odd, col_a, col_b, s, start, size):
    keep = first_half((size, 2 * HALO))
    a, b = col_a[s, pl.ds(start, size)], col_b[s, pl.ds(start, size)]
    w, e = either(col_odd, b, a), either(col_odd, a, b)
    zero = jnp.zeros_like(w)
    wr, er = pltpu.roll(w, HALO, 1), pltpu.roll(e, HALO, 1)
    return (
        (jnp.where(keep, w, zero), jnp.where(keep, zero, er)),
        (jnp.where(keep, wr, zero), jnp.where(keep, zero, e)),
    )


def add_margins(facts, north, south, corners_a, corners_b, row_a, row_b):
    row_odd, col_odd = facts[3], facts[4]
    for s in range(2):
        upper = edge_columns(col_odd, corners_a, corners_b, s, 0, HALO)
        lower = edge_columns(col_odd, corners_a, corners_b, s, HALO, HALO)
        for k in range(2):
            for half, cols in enumerate((slice(0, 128), slice(128, 256))):
                up = north[s, k, :, cols] + upper[k][half]
                down = south[s, k, :, cols] + lower[k][half]
                row_a[s, k, :, cols] = either(row_odd, down, up)
                row_b[s, k, :, cols] = either(row_odd, up, down)


def finish(facts, center, col_a, col_b, row_a, row_b, new_objects):
    row_odd, col_odd = facts[3], facts[4]
    for s in range(2):
        for k, edges in enumerate(edge_columns(col_odd, col_a, col_b, s, 0, TILE)):
            for cols, edge in zip((slice(0, 128), slice(128, 256)), edges):
                value = center[s, k, :, cols] + edge
                a, b = row_a[s, k, :, cols], row_b[s, k, :, cols]
                new_objects[s, k, :HALO, cols] = value[:HALO] + either(row_odd, b, a)
                new_objects[s, k, HALO : TILE - HALO, cols] = value[HALO : TILE - HALO]
                new_objects[s, k, TILE - HALO :, cols] = value[TILE - HALO :] + either(row_odd, a, b)


def call(body, outs, *args, specs=None, scratch=(), flops=0, limit=2, name=None):
    moved = sum(math.prod(o) * 4 for o in outs)
    return pl.pallas_call(
        body,
        out_shape=[jax.ShapeDtypeStruct(o, jnp.float32) for o in outs],
        in_specs=[SMEM] + (specs or [VMEM] * (len(args) - 1)),
        out_specs=[HBM if specs else VMEM] * len(outs),
        scratch_shapes=scratch,
        compiler_params=pltpu.CompilerParams(vmem_limit_bytes=limit * MIB),
        cost_estimate=pl.CostEstimate(flops=flops, bytes_accessed=2 * moved, transcendentals=0),
        name=name,
    )(*args)


def exchanged(value, axis, first):
    pairs = [(i, i + 1) for i in range(first, lax.axis_size(axis) - 1, 2)]
    return lax.ppermute(value, axis, pairs + [(j, i) for i, j in pairs])


def swap(value, axes):
    return lax.all_to_all(value, axes, 0, 0, tiled=True)


def after(value, *others):
    return lax.optimization_barrier((value, *others))[0]


def scatter_sum(partial):
    plane = lax.axis_size(PLANE)
    core = lax.axis_index(PAIR)
    own, other = (lax.dynamic_index_in_dim(partial, k, 0, False) for k in (core, 1 - core))
    part = own + exchanged(other, PAIR, 0)
    return swap(part.reshape(plane, WIN // plane, WIN), PLANE)


def depth_sum(parts, mark):
    part = jnp.sum(after(parts, mark), axis=0)
    return swap(jnp.broadcast_to(part, (lax.axis_size(DEPTH),) + part.shape), DEPTH)


def gather_sum(parts, last):
    part = jnp.sum(parts, axis=0)
    core = lax.axis_index(PAIR)
    own = swap(jnp.broadcast_to(part, (lax.axis_size(PLANE),) + part.shape), PLANE).reshape(WIN, WIN)
    own = after(own, last)
    other = exchanged(own, PAIR, 0)
    return jnp.stack([either(core, own, other), either(core, other, own)])


def shards(objects, probe, prev_partial, offsets, counts, amplitudes):
    strip, column, corners = (2, 2, HALO, TILE), (2, TILE, 2 * HALO), (2, 2 * HALO, 2 * HALO)
    tile = (2, 2, TILE, TILE)
    facts = jnp.concatenate([
        offsets.reshape(2), counts.reshape(1),
        jnp.stack([lax.axis_index("row_2"), lax.axis_index("col_1") % 2]).astype(jnp.int32),
    ])
    row_a, row_b, col_a, col_b = call(pack_sides, [strip] * 2 + [column] * 2, facts, objects, name="pack_sides")
    row_b, row_a = exchanged(row_b, ROW, 1), exchanged(row_a, ROW, 0)
    col_b, col_a = exchanged(col_b, COL, 1), exchanged(col_a, COL, 0)
    scattered = scatter_sum(prev_partial[0, 0])
    sent_a, sent_b = call(pack_corners, [corners] * 2, facts, row_a, row_b, name="pack_corners")
    corners_b, corners_a = exchanged(sent_b, COL, 1), exchanged(sent_a, COL, 0)
    deep = depth_sum(scattered, col_a)
    corners_a, deep = lax.optimization_barrier((corners_a, deep))
    center, north, south, col_a_part, col_b_part, corners_a_part, corners_b_part, partial = call(
        gradient,
        [tile, strip, strip, column, column, corners, corners, (2, WIN, WIN)],
        facts, objects, row_a, row_b, col_a, col_b, corners_a, corners_b, probe,
        amplitudes.reshape(WIN, WIN), jnp.asarray(operator_parts()),
        specs=[ANY] * 3 + [HBM] * 7,
        scratch=[pltpu.VMEM((2, 2, SIDE + 8, SIDE), jnp.float32)] * 2
        + [pltpu.VMEM((2, 2, SIDE, 2 * HALO), jnp.float32)] * 2
        + [pltpu.VMEM((2, WIN, WIN), jnp.float32), pltpu.VMEM((WIN, WIN), jnp.float32)]
        + [pltpu.VMEM((12, WIN, WIN), jnp.bfloat16), pltpu.VMEM((2, WIN, WIN), jnp.float32)]
        + [pltpu.SemaphoreType.DMA((12,)), pltpu.SemaphoreType.DMA((10,))],
        flops=96 * 2 * WIN**3,
        limit=60,
        name="gradient",
    )
    corners_b, corners_a = exchanged(corners_b_part, COL, 1), exchanged(corners_a_part, COL, 0)
    corners_a, corners_b, col_a_part, col_b_part = lax.optimization_barrier(
        (corners_a, corners_b, col_a_part, col_b_part)
    )
    row_a, row_b = call(add_margins, [strip] * 2, facts, north, south, corners_a, corners_b, name="margins")
    row_b, row_a = exchanged(row_b, ROW, 1), exchanged(row_a, ROW, 0)
    col_b, col_a = exchanged(col_b_part, COL, 1), exchanged(col_a_part, COL, 0)
    (new_objects,) = call(finish, [tile], facts, center, col_a, col_b, row_a, row_b, name="finish")
    rate = PROBE_RATE / math.sqrt(lax.axis_size(ROW) * lax.axis_size(COL))
    total = gather_sum(deep, partial)
    new_probe = probe - rate * total
    return (new_objects, new_probe, partial[None, None])


def solution(mesh):
    split = Mesh(mesh.devices.reshape(2, 4, 2, 4, 4), AXES)
    return jax.shard_map(
        shards,
        mesh=split,
        in_specs=(
            P(None, None, ROW, COL),
            P(),
            P(ROW, COL, None, None, None),
            P(ROW, COL, None, None),
            P(ROW, COL),
            P(ROW, COL, None, None, None),
        ),
        out_specs=(P(None, None, ROW, COL), P(), P(ROW, COL, None, None, None)),
        check_vma=False,
    )
```

```python
import math

import jax
import jax.numpy as jnp
import ml_dtypes
import numpy as np
from jax import lax
from jax.experimental import pallas as pl
from jax.experimental.pallas import tpu as pltpu
from jax.sharding import Mesh
from jax.sharding import PartitionSpec as P

WIN = 256
HALO = 64
TILE = 256
SIDE = TILE + 2 * HALO
AXES = ("row_0", "row_1", "row_2", "col_0", "col_1")
ROW = ("row_0", "row_1", "row_2")
COL = ("col_0", "col_1")
PLANE = ("row_1", "col_1")
PAIR = "row_2"
DEPTH = ("row_0", "col_0")

OBJ_RATE = 0.1
PROBE_RATE = 0.3
VMEM = pl.BlockSpec(memory_space=pltpu.VMEM)
HBM = pl.BlockSpec(memory_space=pltpu.HBM)
ANY = pl.BlockSpec(memory_space=pl.ANY)
SMEM = pl.BlockSpec(memory_space=pltpu.SMEM)
MIB = 1024 * 1024


def operator_parts():
    index = np.arange(WIN)
    angle = 2.0 * np.pi * (index[:, None] * index[None, :] % WIN) / WIN
    forward = np.exp(-1j * angle) / math.sqrt(WIN)
    freq = np.where(index < WIN // 2, index, index - WIN)
    shift = np.exp(1j * np.pi * freq.astype(np.float64) ** 2 / (4.0 * WIN))
    propagate = np.conj(forward) @ (shift[:, None] * forward)
    parts = []
    for matrix in (propagate, forward):
        matrix = (matrix + matrix.T) / 2
        halves = []
        for part in (matrix.real, matrix.imag, -matrix.imag):
            high = part.astype(np.float32).astype(ml_dtypes.bfloat16)
            low = (part - high.astype(np.float64)).astype(np.float32)
            halves.append((high, low.astype(ml_dtypes.bfloat16)))
        parts += [high for high, _ in halves] + [low for _, low in halves]
    return np.stack(parts)


def halves_of(value):
    high = value.astype(jnp.bfloat16)
    low = (value - high.astype(jnp.float32)).astype(jnp.bfloat16)
    return high, low


def dot(left, right):
    return jnp.dot(left, right, preferred_element_type=jnp.float32)


def three(left, right):
    (left_high, left_low), (right_high, right_low) = left, right
    return dot(left_high, right_high) + (dot(left_low, right_high) + dot(left_high, right_low))


def sandwich(mats, which, real_part, imag_part):
    def block(rows):
        return jnp.concatenate(
            [jnp.concatenate([mats[6 * which + k] for k in row], axis=1) for row in rows], axis=0
        )

    right = tuple(block(((3 * h, 3 * h + 1), (3 * h + 2, 3 * h))) for h in range(2))
    left = tuple(block(((3 * h, 3 * h + 2), (3 * h + 1, 3 * h))) for h in range(2))
    inner = three(halves_of(jnp.concatenate([real_part, imag_part], axis=1)), right)
    stacked = jnp.concatenate([inner[:, :WIN], inner[:, WIN:]], axis=0)
    outer = three(left, halves_of(stacked))
    return outer[:WIN], outer[WIN:]


def first_half(shape):
    return lax.broadcasted_iota(jnp.int32, shape, len(shape) - 1) < HALO


def side_columns(src, s, size):
    real, imag = src[s, 0], src[s, 1]
    keep = first_half((size, 2 * HALO))
    return (
        jnp.where(keep, real[:, :128], pltpu.roll(imag[:, :128], HALO, 1)),
        jnp.where(keep, pltpu.roll(real[:, 128:], HALO, 1), imag[:, 128:]),
    )


def either(flag, when_even, when_odd):
    return jnp.where(flag == 0, when_even, when_odd)


def pack_sides(facts, objects, row_a, row_b, col_a, col_b):
    row_odd, col_odd = facts[3], facts[4]
    for s in range(2):
        top, bottom = objects[s, :, :HALO], objects[s, :, TILE - HALO :]
        row_a[s] = either(row_odd, bottom, top)
        row_b[s] = either(row_odd, top, bottom)
        first, last = side_columns(objects, s, TILE)
        col_a[s] = either(col_odd, last, first)
        col_b[s] = either(col_odd, first, last)


def pack_corners(facts, row_a, row_b, col_a, col_b):
    row_odd, col_odd = facts[3], facts[4]
    for s in range(2):
        a, b = side_columns(row_a, s, HALO), side_columns(row_b, s, HALO)
        for rows, when_even, when_odd in ((pl.ds(0, HALO), b, a), (pl.ds(HALO, HALO), a, b)):
            first, last = (either(row_odd, *pair) for pair in zip(when_even, when_odd))
            col_a[s, rows] = either(col_odd, last, first)
            col_b[s, rows] = either(col_odd, first, last)


def gradient(
    facts, objects, row_a, row_b, col_a, col_b, corners_a, corners_b, probe, amp, mats,
    center_out, row_a_out, row_b_out, col_a_out, col_b_out, corners_a_out, corners_b_out, probe_out,
    ext, grad, sides, sides_out, probe_in, amp_in, mats_in, probe_grad, arrive, leave,
):
    row_odd, col_odd = facts[3], facts[4]
    across = pl.ds(0, TILE)
    middle, upper, lower = pl.ds(HALO, TILE), pl.ds(0, HALO), pl.ds(HALO + TILE, HALO)

    def beyond(odd):
        return pl.ds(pl.multiple_of((1 - odd) * (HALO + TILE), HALO), HALO)

    incoming = [
        (objects, ext.at[:, :, middle, across]),
        (row_a, ext.at[:, :, beyond(row_odd), across]),
        (row_b, ext.at[:, :, beyond(1 - row_odd), across]),
        (probe, probe_in),
        (mats, mats_in),
        (amp, amp_in),
    ]
    outgoing = [(probe_grad, probe_out)]
    for side, col, corner, col_out, corner_out in (
        (1 - col_odd, col_a, corners_a, col_a_out, corners_a_out),
        (col_odd, col_b, corners_b, col_b_out, corners_b_out),
    ):
        for rows, src, dst in (
            (upper, corner.at[:, upper], corner_out.at[:, upper]),
            (middle, col, col_out),
            (lower, corner.at[:, pl.ds(HALO, HALO)], corner_out.at[:, pl.ds(HALO, HALO)]),
        ):
            incoming.insert(3, (src, sides.at[side, :, rows]))
            outgoing.append((sides_out.at[side, :, rows], dst))
    outgoing += [
        (grad.at[:, :, beyond(row_odd), across], row_a_out),
        (grad.at[:, :, beyond(1 - row_odd), across], row_b_out),
        (ext.at[:, :, middle, across], center_out),
    ]
    coming = [pltpu.make_async_copy(*pair, arrive.at[i]) for i, pair in enumerate(incoming)]
    going = [pltpu.make_async_copy(*pair, leave.at[i]) for i, pair in enumerate(outgoing)]
    for copy in coming:
        copy.start()
    grad[...] = jnp.zeros_like(grad)
    for copy in coming[:-3]:
        copy.wait()
    keep = first_half((SIDE, 2 * HALO))
    for s in range(2):
        w, e = sides[0, s], sides[1, s]
        ext[s, 0, :SIDE, TILE:] = jnp.where(keep, e, pltpu.roll(w, HALO, 1))
        ext[s, 1, :SIDE, TILE:] = jnp.where(keep, pltpu.roll(e, HALO, 1), w)
    top, left = facts[0], facts[1]
    into = lax.rem(SIDE + HALO - left, SIDE)
    back = lax.rem(SIDE - HALO + left, SIDE)
    low = lax.rem(top, 8)
    rows = pl.ds(pl.multiple_of(top - low, 8), WIN + 8)

    def window(s, k):
        wide = pltpu.roll(ext[s, k, rows, :], into, 1)[:, :WIN]
        return pltpu.roll(wide, lax.rem(WIN + 8 - low, WIN + 8), 0)[:WIN]

    def place(s, k, value):
        tall = jnp.concatenate([value, jnp.zeros((8, WIN), jnp.float32)], axis=0)
        tall = pltpu.roll(tall, low, 0)
        wide = jnp.concatenate([tall, jnp.zeros((WIN + 8, SIDE - WIN), jnp.float32)], axis=1)
        grad[s, k, rows, :] = pltpu.roll(wide, back, 1)

    a_re, a_im, b_re, b_im = window(0, 0), window(0, 1), window(1, 0), window(1, 1)
    coming[-3].wait()
    p_re, p_im = probe_in[0], probe_in[1]
    u_re = p_re * a_re - p_im * a_im
    u_im = p_re * a_im + p_im * a_re
    coming[-2].wait()
    v_re, v_im = sandwich(mats_in, 0, u_re, u_im)
    e_re = v_re * b_re - v_im * b_im
    e_im = v_re * b_im + v_im * b_re
    w_re, w_im = sandwich(mats_in, 1, e_re, e_im)
    coming[-1].wait()
    size = jnp.sqrt(w_re * w_re + w_im * w_im + 1.0)
    live = jnp.where(facts[2] > 0, 2.0, 0.0)
    slope = live * (size - amp_in[...]) / size
    e_re, e_im = sandwich(mats_in, 1, slope * w_re, -slope * w_im)
    place(1, 0, -OBJ_RATE * (e_re * v_re - e_im * v_im))
    place(1, 1, OBJ_RATE * (e_re * v_im + e_im * v_re))
    v_re = e_re * b_re - e_im * b_im
    v_im = e_re * b_im + e_im * b_re
    u_re, u_im = sandwich(mats_in, 0, v_re, v_im)
    place(0, 0, -OBJ_RATE * (u_re * p_re - u_im * p_im))
    place(0, 1, OBJ_RATE * (u_re * p_im + u_im * p_re))
    probe_grad[0] = u_re * a_re - u_im * a_im
    probe_grad[1] = -(u_re * a_im + u_im * a_re)
    for s in range(2):
        real, imag = grad[s, 0, :SIDE, TILE:], grad[s, 1, :SIDE, TILE:]
        sides_out[0, s] = jnp.where(keep, pltpu.roll(real, HALO, 1), imag)
        sides_out[1, s] = jnp.where(keep, real, pltpu.roll(imag, HALO, 1))
    for copy in going[:-1]:
        copy.start()
    for s in range(2):
        for k in range(2):
            ext[s, k, middle, :TILE] = ext[s, k, middle, :TILE] + grad[s, k, middle, :TILE]
    going[-1].start()
    for copy in going:
        copy.wait()


def edge_columns(col_odd, col_a, col_b, s, start, size):
    keep = first_half((size, 2 * HALO))
    a, b = (x[s] if x.shape[1] == size else x[s, pl.ds(start, size)] for x in (col_a, col_b))
    w, e = either(col_odd, b, a), either(col_odd, a, b)
    zero = jnp.zeros_like(w)
    wr, er = pltpu.roll(w, HALO, 1), pltpu.roll(e, HALO, 1)
    return (
        (jnp.where(keep, w, zero), jnp.where(keep, zero, er)),
        (jnp.where(keep, wr, zero), jnp.where(keep, zero, e)),
    )


def relay(facts, corners_a, corners_b, row_a, row_b):
    row_odd = facts[3]
    for side, src in ((0, corners_a), (1, corners_b)):
        for s in range(2):
            upper, lower = src[s, :HALO], src[s, HALO:]
            row_a[side, s] = either(row_odd, lower, upper)
            row_b[side, s] = either(row_odd, upper, lower)


def add_sides(facts, center, col_a, col_b, row_a, row_b, tile):
    row_odd, col_odd = facts[3], facts[4]
    for s in range(2):
        edges = edge_columns(col_odd, col_a, col_b, s, 0, TILE)
        for k in range(2):
            for half, cols in enumerate((slice(0, 128), slice(128, 256))):
                value = center[s, k, :, cols] + edges[k][half]
                a, b = row_a[s, k, :, cols], row_b[s, k, :, cols]
                tile[s, k, :HALO, cols] = value[:HALO] + either(row_odd, b, a)
                tile[s, k, HALO : TILE - HALO, cols] = value[HALO : TILE - HALO]
                tile[s, k, TILE - HALO :, cols] = value[TILE - HALO :] + either(row_odd, a, b)


def add_corners(facts, tile, relayed_a, relayed_b, new_objects):
    row_odd, col_odd = facts[3], facts[4]
    for s in range(2):
        a, b = (edge_columns(col_odd, x[0], x[1], s, 0, HALO) for x in (relayed_a, relayed_b))
        for k in range(2):
            for half, cols in enumerate((slice(0, 128), slice(128, 256))):
                first, last = a[k][half], b[k][half]
                new_objects[s, k, :HALO, cols] = tile[s, k, :HALO, cols] + either(row_odd, last, first)
                new_objects[s, k, HALO : TILE - HALO, cols] = tile[s, k, HALO : TILE - HALO, cols]
                new_objects[s, k, TILE - HALO :, cols] = tile[s, k, TILE - HALO :, cols] + either(row_odd, first, last)


def call(body, outs, *args, specs=None, scratch=(), flops=0, limit=2, name=None):
    moved = sum(math.prod(o) * 4 for o in outs)
    return pl.pallas_call(
        body,
        out_shape=[jax.ShapeDtypeStruct(o, jnp.float32) for o in outs],
        in_specs=[SMEM] + (specs or [VMEM] * (len(args) - 1)),
        out_specs=[HBM if specs else VMEM] * len(outs),
        scratch_shapes=scratch,
        compiler_params=pltpu.CompilerParams(vmem_limit_bytes=limit * MIB),
        cost_estimate=pl.CostEstimate(flops=flops, bytes_accessed=2 * moved, transcendentals=0),
        name=name,
    )(*args)


def exchanged(value, axis, first):
    pairs = [(i, i + 1) for i in range(first, lax.axis_size(axis) - 1, 2)]
    return lax.ppermute(value, axis, pairs + [(j, i) for i, j in pairs])


def swap(value, axes):
    return lax.all_to_all(value, axes, 0, 0, tiled=True)


def after(value, *others):
    return lax.optimization_barrier((value, *others))[0]


def scatter_sum(partial):
    plane = lax.axis_size(PLANE)
    core = lax.axis_index(PAIR)
    own, other = (lax.dynamic_index_in_dim(partial, k, 0, False) for k in (core, 1 - core))
    part = own + exchanged(other, PAIR, 0)
    return swap(part.reshape(plane, WIN // plane, WIN), PLANE)


def depth_sum(parts, mark):
    part = jnp.sum(after(parts, mark), axis=0)
    return swap(jnp.broadcast_to(part, (lax.axis_size(DEPTH),) + part.shape), DEPTH)


def gather_sum(parts, last):
    part = jnp.sum(parts, axis=0)
    core = lax.axis_index(PAIR)
    own = swap(jnp.broadcast_to(part, (lax.axis_size(PLANE),) + part.shape), PLANE).reshape(WIN, WIN)
    own = after(own, last)
    other = exchanged(own, PAIR, 0)
    return jnp.stack([either(core, own, other), either(core, other, own)])


def shards(objects, probe, prev_partial, offsets, counts, amplitudes):
    strip, column, corners = (2, 2, HALO, TILE), (2, TILE, 2 * HALO), (2, 2 * HALO, 2 * HALO)
    tile, strip_corners = (2, 2, TILE, TILE), (2, 2, HALO, 2 * HALO)
    facts = jnp.concatenate([
        offsets.reshape(2), counts.reshape(1),
        jnp.stack([lax.axis_index("row_2"), lax.axis_index("col_1") % 2]).astype(jnp.int32),
    ])
    row_a, row_b, col_a, col_b = call(pack_sides, [strip] * 2 + [column] * 2, facts, objects, name="pack_sides")
    row_b, row_a = exchanged(row_b, ROW, 1), exchanged(row_a, ROW, 0)
    col_b, col_a = exchanged(col_b, COL, 1), exchanged(col_a, COL, 0)
    scattered = scatter_sum(prev_partial[0, 0])
    sent_a, sent_b = call(pack_corners, [corners] * 2, facts, row_a, row_b, name="pack_corners")
    corners_b, corners_a = exchanged(sent_b, COL, 1), exchanged(sent_a, COL, 0)
    deep = depth_sum(scattered, col_a)
    corners_a, deep = lax.optimization_barrier((corners_a, deep))
    center, row_a_part, row_b_part, col_a_part, col_b_part, corners_a_part, corners_b_part, partial = call(
        gradient,
        [tile, strip, strip, column, column, corners, corners, (2, WIN, WIN)],
        facts, objects, row_a, row_b, col_a, col_b, corners_a, corners_b, probe,
        amplitudes.reshape(WIN, WIN), jnp.asarray(operator_parts()),
        specs=[ANY] * 3 + [HBM] * 7,
        scratch=[pltpu.VMEM((2, 2, SIDE + 8, SIDE), jnp.float32)] * 2
        + [pltpu.VMEM((2, 2, SIDE, 2 * HALO), jnp.float32)] * 2
        + [pltpu.VMEM((2, WIN, WIN), jnp.float32), pltpu.VMEM((WIN, WIN), jnp.float32)]
        + [pltpu.VMEM((12, WIN, WIN), jnp.bfloat16), pltpu.VMEM((2, WIN, WIN), jnp.float32)]
        + [pltpu.SemaphoreType.DMA((12,)), pltpu.SemaphoreType.DMA((10,))],
        flops=96 * 2 * WIN**3,
        limit=60,
        name="gradient",
    )
    corners_b, corners_a = exchanged(corners_b_part, COL, 1), exchanged(corners_a_part, COL, 0)
    row_b, row_a = exchanged(row_b_part, ROW, 1), exchanged(row_a_part, ROW, 0)
    sent_a, sent_b = call(relay, [strip_corners] * 2, facts, corners_a, corners_b, name="relay")
    relayed_b, relayed_a = exchanged(sent_b, ROW, 1), exchanged(sent_a, ROW, 0)
    col_b, col_a = exchanged(col_b_part, COL, 1), exchanged(col_a_part, COL, 0)
    (added,) = call(add_sides, [tile], facts, center, col_a, col_b, row_a, row_b, name="add_sides")
    (new_objects,) = call(add_corners, [tile], facts, added, relayed_a, relayed_b, name="add_corners")
    rate = PROBE_RATE / math.sqrt(lax.axis_size(ROW) * lax.axis_size(COL))
    total = gather_sum(deep, partial)
    new_probe = probe - rate * total
    return (new_objects, new_probe, partial[None, None])


def solution(mesh):
    split = Mesh(mesh.devices.reshape(2, 4, 2, 4, 4), AXES)
    return jax.shard_map(
        shards,
        mesh=split,
        in_specs=(
            P(None, None, ROW, COL),
            P(),
            P(ROW, COL, None, None, None),
            P(ROW, COL, None, None),
            P(ROW, COL),
            P(ROW, COL, None, None, None),
        ),
        out_specs=(P(None, None, ROW, COL), P(), P(ROW, COL, None, None, None)),
        check_vma=False,
    )
```

```python
import math

import jax
import jax.numpy as jnp
import ml_dtypes
import numpy as np
from jax import lax
from jax.experimental import pallas as pl
from jax.experimental.pallas import tpu as pltpu
from jax.sharding import Mesh
from jax.sharding import PartitionSpec as P

WIN = 256
HALO = 64
TILE = 256
SIDE = TILE + 2 * HALO
AXES = ("row_0", "row_1", "row_2", "col_0", "col_1")
ROW = ("row_0", "row_1", "row_2")
COL = ("col_0", "col_1")
PLANE = ("row_1", "col_1")
PAIR = "row_2"
DEPTH = ("row_0", "col_0")

OBJ_RATE = 0.1
PROBE_RATE = 0.3
VMEM = pl.BlockSpec(memory_space=pltpu.VMEM)
HBM = pl.BlockSpec(memory_space=pltpu.HBM)
ANY = pl.BlockSpec(memory_space=pl.ANY)
SMEM = pl.BlockSpec(memory_space=pltpu.SMEM)
MIB = 1024 * 1024


def operator_parts():
    index = np.arange(WIN)
    angle = 2.0 * np.pi * (index[:, None] * index[None, :] % WIN) / WIN
    forward = np.exp(-1j * angle) / math.sqrt(WIN)
    freq = np.where(index < WIN // 2, index, index - WIN)
    shift = np.exp(1j * np.pi * freq.astype(np.float64) ** 2 / (4.0 * WIN))
    propagate = np.conj(forward) @ (shift[:, None] * forward)
    parts = []
    for matrix in (propagate, forward):
        matrix = (matrix + matrix.T) / 2
        halves = []
        for part in (matrix.real, matrix.imag, -matrix.imag):
            high = part.astype(np.float32).astype(ml_dtypes.bfloat16)
            low = (part - high.astype(np.float64)).astype(np.float32)
            halves.append((high, low.astype(ml_dtypes.bfloat16)))
        parts += [high for high, _ in halves] + [low for _, low in halves]
    return np.stack(parts)


def halves_of(value):
    high = value.astype(jnp.bfloat16)
    low = (value - high.astype(jnp.float32)).astype(jnp.bfloat16)
    return high, low


def dot(left, right):
    return jnp.dot(left, right, preferred_element_type=jnp.float32)


def three(left, right):
    (left_high, left_low), (right_high, right_low) = left, right
    return dot(left_high, right_high) + (dot(left_low, right_high) + dot(left_high, right_low))


def sandwich(mats, which, real_part, imag_part):
    def block(rows):
        return jnp.concatenate(
            [jnp.concatenate([mats[6 * which + k] for k in row], axis=1) for row in rows], axis=0
        )

    right = tuple(block(((3 * h, 3 * h + 1), (3 * h + 2, 3 * h))) for h in range(2))
    left = tuple(block(((3 * h, 3 * h + 2), (3 * h + 1, 3 * h))) for h in range(2))
    inner = three(halves_of(jnp.concatenate([real_part, imag_part], axis=1)), right)
    stacked = jnp.concatenate([inner[:, :WIN], inner[:, WIN:]], axis=0)
    outer = three(left, halves_of(stacked))
    return outer[:WIN], outer[WIN:]


def first_half(shape):
    return lax.broadcasted_iota(jnp.int32, shape, len(shape) - 1) < HALO


def side_columns(src, s, size):
    real, imag = src[s, 0], src[s, 1]
    keep = first_half((size, 2 * HALO))
    return (
        jnp.where(keep, real[:, :128], pltpu.roll(imag[:, :128], HALO, 1)),
        jnp.where(keep, pltpu.roll(real[:, 128:], HALO, 1), imag[:, 128:]),
    )


def either(flag, when_even, when_odd):
    return jnp.where(flag == 0, when_even, when_odd)


def pack_sides(facts, objects, row_a, row_b, col_a, col_b):
    row_odd, col_odd = facts[3], facts[4]
    for s in range(2):
        top, bottom = objects[s, :, :HALO], objects[s, :, TILE - HALO :]
        row_a[s] = either(row_odd, bottom, top)
        row_b[s] = either(row_odd, top, bottom)
        first, last = side_columns(objects, s, TILE)
        col_a[s] = either(col_odd, last, first)
        col_b[s] = either(col_odd, first, last)


def pack_corners(facts, row_a, row_b, col_a, col_b):
    row_odd, col_odd = facts[3], facts[4]
    for s in range(2):
        a, b = side_columns(row_a, s, HALO), side_columns(row_b, s, HALO)
        for rows, when_even, when_odd in ((pl.ds(0, HALO), b, a), (pl.ds(HALO, HALO), a, b)):
            first, last = (either(row_odd, *pair) for pair in zip(when_even, when_odd))
            col_a[s, rows] = either(col_odd, last, first)
            col_b[s, rows] = either(col_odd, first, last)


def gradient(
    facts, objects, row_a, row_b, col_a, col_b, corners_a, corners_b, probe, amp, mats,
    center_out, row_a_out, row_b_out, col_a_out, col_b_out, probe_out,
    ext, grad, sides, sides_out, probe_in, amp_in, mats_in, probe_grad, arrive, leave,
):
    row_odd, col_odd = facts[3], facts[4]
    across = pl.ds(0, TILE)
    middle, upper, lower = pl.ds(HALO, TILE), pl.ds(0, HALO), pl.ds(HALO + TILE, HALO)

    def beyond(odd):
        return pl.ds(pl.multiple_of((1 - odd) * (HALO + TILE), HALO), HALO)

    incoming = [
        (objects, ext.at[:, :, middle, across]),
        (row_a, ext.at[:, :, beyond(row_odd), across]),
        (row_b, ext.at[:, :, beyond(1 - row_odd), across]),
        (probe, probe_in),
        (mats, mats_in),
        (amp, amp_in),
    ]
    for side, col, corner in ((1 - col_odd, col_a, corners_a), (col_odd, col_b, corners_b)):
        for rows, src in (
            (upper, corner.at[:, upper]),
            (middle, col),
            (lower, corner.at[:, pl.ds(HALO, HALO)]),
        ):
            incoming.insert(3, (src, sides.at[side, :, rows]))
    outgoing = [
        (probe_grad, probe_out),
        (sides_out.at[1 - col_odd], col_a_out),
        (sides_out.at[col_odd], col_b_out),
        (grad.at[:, :, beyond(row_odd), across], row_a_out),
        (grad.at[:, :, beyond(1 - row_odd), across], row_b_out),
        (ext.at[:, :, middle, across], center_out),
    ]
    coming = [pltpu.make_async_copy(*pair, arrive.at[i]) for i, pair in enumerate(incoming)]
    going = [pltpu.make_async_copy(*pair, leave.at[i]) for i, pair in enumerate(outgoing)]
    for copy in coming:
        copy.start()
    grad[...] = jnp.zeros_like(grad)
    for copy in coming[:-3]:
        copy.wait()
    keep = first_half((SIDE, 2 * HALO))
    for s in range(2):
        w, e = sides[0, s], sides[1, s]
        ext[s, 0, :SIDE, TILE:] = jnp.where(keep, e, pltpu.roll(w, HALO, 1))
        ext[s, 1, :SIDE, TILE:] = jnp.where(keep, pltpu.roll(e, HALO, 1), w)
    top, left = facts[0], facts[1]
    into = lax.rem(SIDE + HALO - left, SIDE)
    back = lax.rem(SIDE - HALO + left, SIDE)
    low = lax.rem(top, 8)
    rows = pl.ds(pl.multiple_of(top - low, 8), WIN + 8)

    def window(s, k):
        wide = pltpu.roll(ext[s, k, rows, :], into, 1)[:, :WIN]
        return pltpu.roll(wide, lax.rem(WIN + 8 - low, WIN + 8), 0)[:WIN]

    def place(s, k, value):
        tall = jnp.concatenate([value, jnp.zeros((8, WIN), jnp.float32)], axis=0)
        tall = pltpu.roll(tall, low, 0)
        wide = jnp.concatenate([tall, jnp.zeros((WIN + 8, SIDE - WIN), jnp.float32)], axis=1)
        grad[s, k, rows, :] = pltpu.roll(wide, back, 1)

    a_re, a_im, b_re, b_im = window(0, 0), window(0, 1), window(1, 0), window(1, 1)
    coming[-3].wait()
    p_re, p_im = probe_in[0], probe_in[1]
    u_re = p_re * a_re - p_im * a_im
    u_im = p_re * a_im + p_im * a_re
    coming[-2].wait()
    v_re, v_im = sandwich(mats_in, 0, u_re, u_im)
    e_re = v_re * b_re - v_im * b_im
    e_im = v_re * b_im + v_im * b_re
    w_re, w_im = sandwich(mats_in, 1, e_re, e_im)
    coming[-1].wait()
    size = jnp.sqrt(w_re * w_re + w_im * w_im + 1.0)
    live = jnp.where(facts[2] > 0, 2.0, 0.0)
    slope = live * (size - amp_in[...]) / size
    e_re, e_im = sandwich(mats_in, 1, slope * w_re, -slope * w_im)
    place(1, 0, -OBJ_RATE * (e_re * v_re - e_im * v_im))
    place(1, 1, OBJ_RATE * (e_re * v_im + e_im * v_re))
    v_re = e_re * b_re - e_im * b_im
    v_im = e_re * b_im + e_im * b_re
    u_re, u_im = sandwich(mats_in, 0, v_re, v_im)
    place(0, 0, -OBJ_RATE * (u_re * p_re - u_im * p_im))
    place(0, 1, OBJ_RATE * (u_re * p_im + u_im * p_re))
    probe_grad[0] = u_re * a_re - u_im * a_im
    probe_grad[1] = -(u_re * a_im + u_im * a_re)
    for s in range(2):
        real, imag = grad[s, 0, :SIDE, TILE:], grad[s, 1, :SIDE, TILE:]
        sides_out[0, s] = jnp.where(keep, pltpu.roll(real, HALO, 1), imag)
        sides_out[1, s] = jnp.where(keep, real, pltpu.roll(imag, HALO, 1))
    for copy in going[:-1]:
        copy.start()
    for s in range(2):
        for k in range(2):
            ext[s, k, middle, :TILE] = ext[s, k, middle, :TILE] + grad[s, k, middle, :TILE]
    going[-1].start()
    for copy in going:
        copy.wait()


def edge_columns(col_odd, col_a, col_b, s, start, size):
    keep = first_half((size, 2 * HALO))
    a, b = (x[s] if x.shape[1] == size else x[s, pl.ds(start, size)] for x in (col_a, col_b))
    w, e = either(col_odd, b, a), either(col_odd, a, b)
    zero = jnp.zeros_like(w)
    wr, er = pltpu.roll(w, HALO, 1), pltpu.roll(e, HALO, 1)
    return (
        (jnp.where(keep, w, zero), jnp.where(keep, zero, er)),
        (jnp.where(keep, wr, zero), jnp.where(keep, zero, e)),
    )


def relay(facts, col_a, col_b, row_a, row_b):
    row_odd = facts[3]
    for side, src in ((0, col_a), (1, col_b)):
        for s in range(2):
            upper, lower = src[s, :HALO], src[s, HALO + TILE :]
            row_a[side, s] = either(row_odd, lower, upper)
            row_b[side, s] = either(row_odd, upper, lower)


def add_sides(facts, center, col_a, col_b, row_a, row_b, tile):
    row_odd, col_odd = facts[3], facts[4]
    for s in range(2):
        edges = edge_columns(col_odd, col_a, col_b, s, HALO, TILE)
        for k in range(2):
            for half, cols in enumerate((slice(0, 128), slice(128, 256))):
                value = center[s, k, :, cols] + edges[k][half]
                a, b = row_a[s, k, :, cols], row_b[s, k, :, cols]
                tile[s, k, :HALO, cols] = value[:HALO] + either(row_odd, b, a)
                tile[s, k, HALO : TILE - HALO, cols] = value[HALO : TILE - HALO]
                tile[s, k, TILE - HALO :, cols] = value[TILE - HALO :] + either(row_odd, a, b)


def add_corners(facts, tile, relayed_a, relayed_b, new_objects):
    row_odd, col_odd = facts[3], facts[4]
    for s in range(2):
        a, b = (edge_columns(col_odd, x[0], x[1], s, 0, HALO) for x in (relayed_a, relayed_b))
        for k in range(2):
            for half, cols in enumerate((slice(0, 128), slice(128, 256))):
                first, last = a[k][half], b[k][half]
                new_objects[s, k, :HALO, cols] = tile[s, k, :HALO, cols] + either(row_odd, last, first)
                new_objects[s, k, HALO : TILE - HALO, cols] = tile[s, k, HALO : TILE - HALO, cols]
                new_objects[s, k, TILE - HALO :, cols] = tile[s, k, TILE - HALO :, cols] + either(row_odd, first, last)


def call(body, outs, *args, specs=None, scratch=(), flops=0, limit=2, name=None):
    moved = sum(math.prod(o) * 4 for o in outs)
    return pl.pallas_call(
        body,
        out_shape=[jax.ShapeDtypeStruct(o, jnp.float32) for o in outs],
        in_specs=[SMEM] + (specs or [VMEM] * (len(args) - 1)),
        out_specs=[HBM if specs else VMEM] * len(outs),
        scratch_shapes=scratch,
        compiler_params=pltpu.CompilerParams(vmem_limit_bytes=limit * MIB),
        cost_estimate=pl.CostEstimate(flops=flops, bytes_accessed=2 * moved, transcendentals=0),
        name=name,
    )(*args)


def exchanged(value, axis, first):
    pairs = [(i, i + 1) for i in range(first, lax.axis_size(axis) - 1, 2)]
    return lax.ppermute(value, axis, pairs + [(j, i) for i, j in pairs])


def swap(value, axes):
    return lax.all_to_all(value, axes, 0, 0, tiled=True)


def after(value, *others):
    return lax.optimization_barrier((value, *others))[0]


def scatter_sum(partial):
    plane = lax.axis_size(PLANE)
    core = lax.axis_index(PAIR)
    own, other = (lax.dynamic_index_in_dim(partial, k, 0, False) for k in (core, 1 - core))
    part = own + exchanged(other, PAIR, 0)
    return swap(part.reshape(plane, WIN // plane, WIN), PLANE)


def depth_sum(parts, mark):
    part = jnp.sum(after(parts, mark), axis=0)
    return swap(jnp.broadcast_to(part, (lax.axis_size(DEPTH),) + part.shape), DEPTH)


def gather_sum(parts, last):
    part = jnp.sum(parts, axis=0)
    core = lax.axis_index(PAIR)
    own = swap(jnp.broadcast_to(part, (lax.axis_size(PLANE),) + part.shape), PLANE).reshape(WIN, WIN)
    own = after(own, last)
    other = exchanged(own, PAIR, 0)
    return jnp.stack([either(core, own, other), either(core, other, own)])


def shards(objects, probe, prev_partial, offsets, counts, amplitudes):
    strip, column, corners = (2, 2, HALO, TILE), (2, TILE, 2 * HALO), (2, 2 * HALO, 2 * HALO)
    tile, strip_corners = (2, 2, TILE, TILE), (2, 2, HALO, 2 * HALO)
    whole_column = (2, SIDE, 2 * HALO)
    facts = jnp.concatenate([
        offsets.reshape(2), counts.reshape(1),
        jnp.stack([lax.axis_index("row_2"), lax.axis_index("col_1") % 2]).astype(jnp.int32),
    ])
    row_a, row_b, col_a, col_b = call(pack_sides, [strip] * 2 + [column] * 2, facts, objects, name="pack_sides")
    row_b, row_a = exchanged(row_b, ROW, 1), exchanged(row_a, ROW, 0)
    col_b, col_a = exchanged(col_b, COL, 1), exchanged(col_a, COL, 0)
    scattered = scatter_sum(prev_partial[0, 0])
    sent_a, sent_b = call(pack_corners, [corners] * 2, facts, row_a, row_b, name="pack_corners")
    corners_b, corners_a = exchanged(sent_b, COL, 1), exchanged(sent_a, COL, 0)
    deep = depth_sum(scattered, col_a)
    corners_a, deep = lax.optimization_barrier((corners_a, deep))
    center, row_a_part, row_b_part, col_a_part, col_b_part, partial = call(
        gradient,
        [tile, strip, strip, whole_column, whole_column, (2, WIN, WIN)],
        facts, objects, row_a, row_b, col_a, col_b, corners_a, corners_b, probe,
        amplitudes.reshape(WIN, WIN), jnp.asarray(operator_parts()),
        specs=[ANY] * 3 + [HBM] * 7,
        scratch=[pltpu.VMEM((2, 2, SIDE + 8, SIDE), jnp.float32)] * 2
        + [pltpu.VMEM((2, 2, SIDE, 2 * HALO), jnp.float32)] * 2
        + [pltpu.VMEM((2, WIN, WIN), jnp.float32), pltpu.VMEM((WIN, WIN), jnp.float32)]
        + [pltpu.VMEM((12, WIN, WIN), jnp.bfloat16), pltpu.VMEM((2, WIN, WIN), jnp.float32)]
        + [pltpu.SemaphoreType.DMA((12,)), pltpu.SemaphoreType.DMA((6,))],
        flops=96 * 2 * WIN**3,
        limit=60,
        name="gradient",
    )
    col_b, col_a = exchanged(col_b_part, COL, 1), exchanged(col_a_part, COL, 0)
    row_b, row_a = exchanged(row_b_part, ROW, 1), exchanged(row_a_part, ROW, 0)
    sent_a, sent_b = call(relay, [strip_corners] * 2, facts, col_a, col_b, name="relay")
    relayed_b, relayed_a = exchanged(sent_b, ROW, 1), exchanged(sent_a, ROW, 0)
    (added,) = call(add_sides, [tile], facts, center, col_a, col_b, row_a, row_b, name="add_sides")
    (new_objects,) = call(add_corners, [tile], facts, added, relayed_a, relayed_b, name="add_corners")
    rate = PROBE_RATE / math.sqrt(lax.axis_size(ROW) * lax.axis_size(COL))
    total = gather_sum(deep, partial)
    new_probe = probe - rate * total
    return (new_objects, new_probe, partial[None, None])


def solution(mesh):
    split = Mesh(mesh.devices.reshape(2, 4, 2, 4, 4), AXES)
    return jax.shard_map(
        shards,
        mesh=split,
        in_specs=(
            P(None, None, ROW, COL),
            P(),
            P(ROW, COL, None, None, None),
            P(ROW, COL, None, None),
            P(ROW, COL),
            P(ROW, COL, None, None, None),
        ),
        out_specs=(P(None, None, ROW, COL), P(), P(ROW, COL, None, None, None)),
        check_vma=False,
    )
```

```python
import math

import jax
import jax.numpy as jnp
import ml_dtypes
import numpy as np
from jax import lax
from jax.experimental import pallas as pl
from jax.experimental.pallas import tpu as pltpu
from jax.sharding import Mesh
from jax.sharding import PartitionSpec as P

WIN = 256
HALO = 64
TILE = 256
SIDE = TILE + 2 * HALO
AXES = ("row_0", "row_1", "row_2", "col_0", "col_1")
ROW = ("row_0", "row_1", "row_2")
COL = ("col_0", "col_1")
PLANE = ("row_1", "col_1")
PAIR = "row_2"
DEPTH = ("row_0", "col_0")

OBJ_RATE = 0.1
PROBE_RATE = 0.3
VMEM = pl.BlockSpec(memory_space=pltpu.VMEM)
HBM = pl.BlockSpec(memory_space=pltpu.HBM)
ANY = pl.BlockSpec(memory_space=pl.ANY)
SMEM = pl.BlockSpec(memory_space=pltpu.SMEM)
MIB = 1024 * 1024


def operator_parts():
    index = np.arange(WIN)
    angle = 2.0 * np.pi * (index[:, None] * index[None, :] % WIN) / WIN
    forward = np.exp(-1j * angle) / math.sqrt(WIN)
    freq = np.where(index < WIN // 2, index, index - WIN)
    shift = np.exp(1j * np.pi * freq.astype(np.float64) ** 2 / (4.0 * WIN))
    propagate = np.conj(forward) @ (shift[:, None] * forward)
    parts = []
    for matrix in (propagate, forward):
        matrix = (matrix + matrix.T) / 2
        halves = []
        for part in (matrix.real, matrix.imag, -matrix.imag):
            high = part.astype(np.float32).astype(ml_dtypes.bfloat16)
            low = (part - high.astype(np.float64)).astype(np.float32)
            halves.append((high, low.astype(ml_dtypes.bfloat16)))
        parts += [high for high, _ in halves] + [low for _, low in halves]
    return np.stack(parts)


def halves_of(value):
    high = value.astype(jnp.bfloat16)
    low = (value - high.astype(jnp.float32)).astype(jnp.bfloat16)
    return high, low


def dot(left, right):
    return jnp.dot(left, right, preferred_element_type=jnp.float32)


def three(left, right):
    (left_high, left_low), (right_high, right_low) = left, right
    return dot(left_high, right_high) + (dot(left_low, right_high) + dot(left_high, right_low))


def sandwich(mats, which, real_part, imag_part):
    def block(rows):
        return jnp.concatenate(
            [jnp.concatenate([mats[6 * which + k] for k in row], axis=1) for row in rows], axis=0
        )

    right = tuple(block(((3 * h, 3 * h + 1), (3 * h + 2, 3 * h))) for h in range(2))
    left = tuple(block(((3 * h, 3 * h + 2), (3 * h + 1, 3 * h))) for h in range(2))
    inner = three(halves_of(jnp.concatenate([real_part, imag_part], axis=1)), right)
    stacked = jnp.concatenate([inner[:, :WIN], inner[:, WIN:]], axis=0)
    outer = three(left, halves_of(stacked))
    return outer[:WIN], outer[WIN:]


def first_half(shape):
    return lax.broadcasted_iota(jnp.int32, shape, len(shape) - 1) < HALO


def side_columns(src, s, size):
    real, imag = src[s, 0], src[s, 1]
    keep = first_half((size, 2 * HALO))
    return (
        jnp.where(keep, real[:, :128], pltpu.roll(imag[:, :128], HALO, 1)),
        jnp.where(keep, pltpu.roll(real[:, 128:], HALO, 1), imag[:, 128:]),
    )


def either(flag, when_even, when_odd):
    return jnp.where(flag == 0, when_even, when_odd)


def pack_sides(facts, objects, row_a, row_b, col_a, col_b):
    row_odd, col_odd = facts[3], facts[4]
    for s in range(2):
        top, bottom = objects[s, :, :HALO], objects[s, :, TILE - HALO :]
        row_a[s] = either(row_odd, bottom, top)
        row_b[s] = either(row_odd, top, bottom)
        first, last = side_columns(objects, s, TILE)
        col_a[s] = either(col_odd, last, first)
        col_b[s] = either(col_odd, first, last)


def pack_corners(facts, row_a, row_b, col_a, col_b):
    row_odd, col_odd = facts[3], facts[4]
    for s in range(2):
        a, b = side_columns(row_a, s, HALO), side_columns(row_b, s, HALO)
        for rows, when_even, when_odd in ((pl.ds(0, HALO), b, a), (pl.ds(HALO, HALO), a, b)):
            first, last = (either(row_odd, *pair) for pair in zip(when_even, when_odd))
            col_a[s, rows] = either(col_odd, last, first)
            col_b[s, rows] = either(col_odd, first, last)


def gradient(
    facts, objects, row_a, row_b, col_a, col_b, corners_a, corners_b, probe, amp, mats,
    center_out, row_a_out, row_b_out, col_a_out, col_b_out, probe_out,
    ext, grad, sides, sides_out, probe_in, amp_in, mats_in, probe_grad, arrive, leave,
):
    row_odd, col_odd = facts[3], facts[4]
    across = pl.ds(0, TILE)
    middle, upper, lower = pl.ds(HALO, TILE), pl.ds(0, HALO), pl.ds(HALO + TILE, HALO)

    def beyond(odd):
        return pl.ds(pl.multiple_of((1 - odd) * (HALO + TILE), HALO), HALO)

    incoming = [
        (objects, ext.at[:, :, middle, across]),
        (row_a, ext.at[:, :, beyond(row_odd), across]),
        (row_b, ext.at[:, :, beyond(1 - row_odd), across]),
        (probe, probe_in),
        (mats, mats_in),
        (amp, amp_in),
    ]
    for side, col, corner in ((1 - col_odd, col_a, corners_a), (col_odd, col_b, corners_b)):
        for rows, src in (
            (upper, corner.at[:, upper]),
            (middle, col),
            (lower, corner.at[:, pl.ds(HALO, HALO)]),
        ):
            incoming.insert(3, (src, sides.at[side, :, rows]))
    outgoing = [
        (probe_grad, probe_out),
        (sides_out.at[1 - col_odd], col_a_out),
        (sides_out.at[col_odd], col_b_out),
        (grad.at[:, :, beyond(row_odd), across], row_a_out),
        (grad.at[:, :, beyond(1 - row_odd), across], row_b_out),
        (ext.at[:, :, middle, across], center_out),
    ]
    coming = [pltpu.make_async_copy(*pair, arrive.at[i]) for i, pair in enumerate(incoming)]
    going = [pltpu.make_async_copy(*pair, leave.at[i]) for i, pair in enumerate(outgoing)]
    for copy in coming:
        copy.start()
    grad[...] = jnp.zeros_like(grad)
    for copy in coming[:-3]:
        copy.wait()
    keep = first_half((SIDE, 2 * HALO))
    for s in range(2):
        w, e = sides[0, s], sides[1, s]
        ext[s, 0, :SIDE, TILE:] = jnp.where(keep, e, pltpu.roll(w, HALO, 1))
        ext[s, 1, :SIDE, TILE:] = jnp.where(keep, pltpu.roll(e, HALO, 1), w)
    top, left = facts[0], facts[1]
    into = lax.rem(SIDE + HALO - left, SIDE)
    back = lax.rem(SIDE - HALO + left, SIDE)
    low = lax.rem(top, 8)
    rows = pl.ds(pl.multiple_of(top - low, 8), WIN + 8)

    def window(s, k):
        wide = pltpu.roll(ext[s, k, rows, :], into, 1)[:, :WIN]
        return pltpu.roll(wide, lax.rem(WIN + 8 - low, WIN + 8), 0)[:WIN]

    def place(s, k, value):
        tall = jnp.concatenate([value, jnp.zeros((8, WIN), jnp.float32)], axis=0)
        tall = pltpu.roll(tall, low, 0)
        wide = jnp.concatenate([tall, jnp.zeros((WIN + 8, SIDE - WIN), jnp.float32)], axis=1)
        grad[s, k, rows, :] = pltpu.roll(wide, back, 1)

    a_re, a_im, b_re, b_im = window(0, 0), window(0, 1), window(1, 0), window(1, 1)
    coming[-3].wait()
    p_re, p_im = probe_in[0], probe_in[1]
    u_re = p_re * a_re - p_im * a_im
    u_im = p_re * a_im + p_im * a_re
    coming[-2].wait()
    v_re, v_im = sandwich(mats_in, 0, u_re, u_im)
    e_re = v_re * b_re - v_im * b_im
    e_im = v_re * b_im + v_im * b_re
    w_re, w_im = sandwich(mats_in, 1, e_re, e_im)
    coming[-1].wait()
    size = jnp.sqrt(w_re * w_re + w_im * w_im + 1.0)
    live = jnp.where(facts[2] > 0, 2.0, 0.0)
    slope = live * (size - amp_in[...]) / size
    e_re, e_im = sandwich(mats_in, 1, slope * w_re, -slope * w_im)
    place(1, 0, -OBJ_RATE * (e_re * v_re - e_im * v_im))
    place(1, 1, OBJ_RATE * (e_re * v_im + e_im * v_re))
    v_re = e_re * b_re - e_im * b_im
    v_im = e_re * b_im + e_im * b_re
    u_re, u_im = sandwich(mats_in, 0, v_re, v_im)
    place(0, 0, -OBJ_RATE * (u_re * p_re - u_im * p_im))
    place(0, 1, OBJ_RATE * (u_re * p_im + u_im * p_re))
    probe_grad[0] = u_re * a_re - u_im * a_im
    probe_grad[1] = -(u_re * a_im + u_im * a_re)
    for s in range(2):
        real, imag = grad[s, 0, :SIDE, TILE:], grad[s, 1, :SIDE, TILE:]
        sides_out[0, s] = jnp.where(keep, pltpu.roll(real, HALO, 1), imag)
        sides_out[1, s] = jnp.where(keep, real, pltpu.roll(imag, HALO, 1))
    for copy in going[:-1]:
        copy.start()
    for s in range(2):
        for k in range(2):
            ext[s, k, middle, :TILE] = ext[s, k, middle, :TILE] + grad[s, k, middle, :TILE]
    going[-1].start()
    for copy in going:
        copy.wait()


def edge_columns(col_odd, col_a, col_b, s, start, size):
    keep = first_half((size, 2 * HALO))
    a, b = (x[s] if x.shape[1] == size else x[s, pl.ds(start, size)] for x in (col_a, col_b))
    w, e = either(col_odd, b, a), either(col_odd, a, b)
    zero = jnp.zeros_like(w)
    wr, er = pltpu.roll(w, HALO, 1), pltpu.roll(e, HALO, 1)
    return (
        (jnp.where(keep, w, zero), jnp.where(keep, zero, er)),
        (jnp.where(keep, wr, zero), jnp.where(keep, zero, e)),
    )


def relay(facts, col_a, col_b, row_a, row_b):
    row_odd = facts[3]
    for side, src in ((0, col_a), (1, col_b)):
        for s in range(2):
            upper, lower = src[s, :HALO], src[s, HALO + TILE :]
            row_a[side, s] = either(row_odd, lower, upper)
            row_b[side, s] = either(row_odd, upper, lower)


def add_sides(facts, center, col_a, col_b, row_a, row_b, tile):
    row_odd, col_odd = facts[3], facts[4]
    for s in range(2):
        edges = edge_columns(col_odd, col_a, col_b, s, HALO, TILE)
        for k in range(2):
            for half, cols in enumerate((slice(0, 128), slice(128, 256))):
                value = center[s, k, :, cols] + edges[k][half]
                a, b = row_a[s, k, :, cols], row_b[s, k, :, cols]
                tile[s, k, :HALO, cols] = value[:HALO] + either(row_odd, b, a)
                tile[s, k, HALO : TILE - HALO, cols] = value[HALO : TILE - HALO]
                tile[s, k, TILE - HALO :, cols] = value[TILE - HALO :] + either(row_odd, a, b)


def add_corners(facts, tile, relayed_a, relayed_b, new_objects):
    row_odd, col_odd = facts[3], facts[4]
    for s in range(2):
        a, b = (edge_columns(col_odd, x[0], x[1], s, 0, HALO) for x in (relayed_a, relayed_b))
        for k in range(2):
            for half, cols in enumerate((slice(0, 128), slice(128, 256))):
                first, last = a[k][half], b[k][half]
                new_objects[s, k, :HALO, cols] = tile[s, k, :HALO, cols] + either(row_odd, last, first)
                new_objects[s, k, HALO : TILE - HALO, cols] = tile[s, k, HALO : TILE - HALO, cols]
                new_objects[s, k, TILE - HALO :, cols] = tile[s, k, TILE - HALO :, cols] + either(row_odd, first, last)


def call(body, outs, *args, specs=None, scratch=(), flops=0, limit=2, name=None):
    moved = sum(math.prod(o) * 4 for o in outs)
    return pl.pallas_call(
        body,
        out_shape=[jax.ShapeDtypeStruct(o, jnp.float32) for o in outs],
        in_specs=[SMEM] + (specs or [VMEM] * (len(args) - 1)),
        out_specs=[HBM if specs else VMEM] * len(outs),
        scratch_shapes=scratch,
        compiler_params=pltpu.CompilerParams(vmem_limit_bytes=limit * MIB),
        cost_estimate=pl.CostEstimate(flops=flops, bytes_accessed=2 * moved, transcendentals=0),
        name=name,
    )(*args)


def exchanged(value, axis, first):
    pairs = [(i, i + 1) for i in range(first, lax.axis_size(axis) - 1, 2)]
    return lax.ppermute(value, axis, pairs + [(j, i) for i, j in pairs])


def swap(value, axes):
    return lax.all_to_all(value, axes, 0, 0, tiled=True)


def after(value, *others):
    return lax.optimization_barrier((value, *others))[0]


def scatter_sum(partial, mark):
    plane = lax.axis_size(PLANE)
    core = lax.axis_index(PAIR)
    own, other = (lax.dynamic_index_in_dim(partial, k, 0, False) for k in (core, 1 - core))
    part = own + exchanged(after(other, mark), PAIR, 0)
    return swap(part.reshape(plane, WIN // plane, WIN), PLANE)


def depth_sum(parts, mark):
    part = jnp.sum(after(parts, mark), axis=0)
    return swap(jnp.broadcast_to(part, (lax.axis_size(DEPTH),) + part.shape), DEPTH)


def gather_sum(parts, mark, last):
    part = jnp.sum(after(parts, mark), axis=0)
    core = lax.axis_index(PAIR)
    own = swap(jnp.broadcast_to(part, (lax.axis_size(PLANE),) + part.shape), PLANE).reshape(WIN, WIN)
    own = after(own, last)
    other = exchanged(own, PAIR, 0)
    return jnp.stack([either(core, own, other), either(core, other, own)])


def shards(objects, probe, prev_partial, offsets, counts, amplitudes):
    strip, column, corners = (2, 2, HALO, TILE), (2, TILE, 2 * HALO), (2, 2 * HALO, 2 * HALO)
    tile, strip_corners = (2, 2, TILE, TILE), (2, 2, HALO, 2 * HALO)
    whole_column = (2, SIDE, 2 * HALO)
    facts = jnp.concatenate([
        offsets.reshape(2), counts.reshape(1),
        jnp.stack([lax.axis_index("row_2"), lax.axis_index("col_1") % 2]).astype(jnp.int32),
    ])
    row_a, row_b, col_a, col_b = call(pack_sides, [strip] * 2 + [column] * 2, facts, objects, name="pack_sides")
    row_b, row_a = exchanged(row_b, ROW, 1), exchanged(row_a, ROW, 0)
    col_b, col_a = exchanged(col_b, COL, 1), exchanged(col_a, COL, 0)
    scattered = scatter_sum(prev_partial[0, 0], row_a)
    sent_a, sent_b = call(pack_corners, [corners] * 2, facts, row_a, row_b, name="pack_corners")
    corners_b, corners_a = exchanged(sent_b, COL, 1), exchanged(sent_a, COL, 0)
    deep = depth_sum(scattered, sent_a)
    corners_a, deep = lax.optimization_barrier((corners_a, deep))
    center, row_a_part, row_b_part, col_a_part, col_b_part, partial = call(
        gradient,
        [tile, strip, strip, whole_column, whole_column, (2, WIN, WIN)],
        facts, objects, row_a, row_b, col_a, col_b, corners_a, corners_b, probe,
        amplitudes.reshape(WIN, WIN), jnp.asarray(operator_parts()),
        specs=[ANY] * 3 + [HBM] * 7,
        scratch=[pltpu.VMEM((2, 2, SIDE + 8, SIDE), jnp.float32)] * 2
        + [pltpu.VMEM((2, 2, SIDE, 2 * HALO), jnp.float32)] * 2
        + [pltpu.VMEM((2, WIN, WIN), jnp.float32), pltpu.VMEM((WIN, WIN), jnp.float32)]
        + [pltpu.VMEM((12, WIN, WIN), jnp.bfloat16), pltpu.VMEM((2, WIN, WIN), jnp.float32)]
        + [pltpu.SemaphoreType.DMA((12,)), pltpu.SemaphoreType.DMA((6,))],
        flops=96 * 2 * WIN**3,
        limit=60,
        name="gradient",
    )
    col_b, col_a = exchanged(col_b_part, COL, 1), exchanged(col_a_part, COL, 0)
    row_b, row_a = exchanged(row_b_part, ROW, 1), exchanged(row_a_part, ROW, 0)
    sent_a, sent_b = call(relay, [strip_corners] * 2, facts, col_a, col_b, name="relay")
    relayed_b, relayed_a = exchanged(sent_b, ROW, 1), exchanged(sent_a, ROW, 0)
    (added,) = call(add_sides, [tile], facts, center, col_a, col_b, row_a, row_b, name="add_sides")
    (new_objects,) = call(add_corners, [tile], facts, added, relayed_a, relayed_b, name="add_corners")
    rate = PROBE_RATE / math.sqrt(lax.axis_size(ROW) * lax.axis_size(COL))
    total = gather_sum(deep, partial, new_objects)
    new_probe = probe - rate * total
    return (new_objects, new_probe, partial[None, None])


def solution(mesh):
    split = Mesh(mesh.devices.reshape(2, 4, 2, 4, 4), AXES)
    return jax.shard_map(
        shards,
        mesh=split,
        in_specs=(
            P(None, None, ROW, COL),
            P(),
            P(ROW, COL, None, None, None),
            P(ROW, COL, None, None),
            P(ROW, COL),
            P(ROW, COL, None, None, None),
        ),
        out_specs=(P(None, None, ROW, COL), P(), P(ROW, COL, None, None, None)),
        check_vma=False,
    )
```

```python
import math

import jax
import jax.numpy as jnp
import ml_dtypes
import numpy as np
from jax import lax
from jax.experimental import pallas as pl
from jax.experimental.pallas import tpu as pltpu
from jax.sharding import Mesh
from jax.sharding import PartitionSpec as P

WIN = 256
HALO = 64
TILE = 256
SIDE = TILE + 2 * HALO
AXES = ("row_0", "row_1", "row_2", "col_0", "col_1")
ROW = ("row_0", "row_1", "row_2")
COL = ("col_0", "col_1")
PLANE = ("row_1", "col_1")
PAIR = "row_2"
DEPTH = ("row_0", "col_0")

OBJ_RATE = 0.1
PROBE_RATE = 0.3
VMEM = pl.BlockSpec(memory_space=pltpu.VMEM)
HBM = pl.BlockSpec(memory_space=pltpu.HBM)
ANY = pl.BlockSpec(memory_space=pl.ANY)
SMEM = pl.BlockSpec(memory_space=pltpu.SMEM)
MIB = 1024 * 1024


def operator_parts():
    index = np.arange(WIN)
    angle = 2.0 * np.pi * (index[:, None] * index[None, :] % WIN) / WIN
    forward = np.exp(-1j * angle) / math.sqrt(WIN)
    freq = np.where(index < WIN // 2, index, index - WIN)
    shift = np.exp(1j * np.pi * freq.astype(np.float64) ** 2 / (4.0 * WIN))
    propagate = np.conj(forward) @ (shift[:, None] * forward)
    parts = []
    for matrix in (propagate, forward):
        matrix = (matrix + matrix.T) / 2
        halves = []
        for part in (matrix.real, matrix.imag, matrix.real + matrix.imag):
            high = part.astype(np.float32).astype(ml_dtypes.bfloat16)
            low = (part - high.astype(np.float64)).astype(np.float32)
            halves.append((high, low.astype(ml_dtypes.bfloat16)))
        parts += [high for high, _ in halves] + [low for _, low in halves]
    return np.stack(parts)


def halves_of(value):
    high = value.astype(jnp.bfloat16)
    low = (value - high.astype(jnp.float32)).astype(jnp.bfloat16)
    return high, low


def dot(left, right):
    return jnp.dot(left, right, preferred_element_type=jnp.float32)


def three(left, right):
    (left_high, left_low), (right_high, right_low) = left, right
    return dot(left_high, right_high) + (dot(left_low, right_high) + dot(left_high, right_low))


def sandwich(mats, which, real_part, imag_part):
    def halves(k):
        return mats[6 * which + k], mats[6 * which + 3 + k]

    def combine(real_real, imag_imag, both):
        return real_real - imag_imag, both - real_real - imag_imag

    parts = (real_part, imag_part, real_part + imag_part)
    real_part, imag_part = combine(*(three(halves_of(part), halves(k)) for k, part in enumerate(parts)))
    parts = (real_part, imag_part, real_part + imag_part)
    return combine(*(three(halves(k), halves_of(part)) for k, part in enumerate(parts)))


def first_half(shape):
    return lax.broadcasted_iota(jnp.int32, shape, len(shape) - 1) < HALO


def side_columns(src, s, size):
    real, imag = src[s, 0], src[s, 1]
    keep = first_half((size, 2 * HALO))
    return (
        jnp.where(keep, real[:, :128], pltpu.roll(imag[:, :128], HALO, 1)),
        jnp.where(keep, pltpu.roll(real[:, 128:], HALO, 1), imag[:, 128:]),
    )


def either(flag, when_even, when_odd):
    return jnp.where(flag == 0, when_even, when_odd)


def pack_sides(facts, objects, row_a, row_b, col_a, col_b):
    row_odd, col_odd = facts[3], facts[4]
    for s in range(2):
        top, bottom = objects[s, :, :HALO], objects[s, :, TILE - HALO :]
        row_a[s] = either(row_odd, bottom, top)
        row_b[s] = either(row_odd, top, bottom)
        first, last = side_columns(objects, s, TILE)
        col_a[s] = either(col_odd, last, first)
        col_b[s] = either(col_odd, first, last)


def pack_corners(facts, row_a, row_b, col_a, col_b):
    row_odd, col_odd = facts[3], facts[4]
    for s in range(2):
        a, b = side_columns(row_a, s, HALO), side_columns(row_b, s, HALO)
        for rows, when_even, when_odd in ((pl.ds(0, HALO), b, a), (pl.ds(HALO, HALO), a, b)):
            first, last = (either(row_odd, *pair) for pair in zip(when_even, when_odd))
            col_a[s, rows] = either(col_odd, last, first)
            col_b[s, rows] = either(col_odd, first, last)


def gradient(
    facts, objects, row_a, row_b, col_a, col_b, corners_a, corners_b, probe, amp, mats,
    center_out, row_a_out, row_b_out, col_a_out, col_b_out, probe_out,
    ext, grad, sides, sides_out, probe_in, amp_in, mats_in, probe_grad, arrive, leave,
):
    row_odd, col_odd = facts[3], facts[4]
    across = pl.ds(0, TILE)
    middle, upper, lower = pl.ds(HALO, TILE), pl.ds(0, HALO), pl.ds(HALO + TILE, HALO)

    def beyond(odd):
        return pl.ds(pl.multiple_of((1 - odd) * (HALO + TILE), HALO), HALO)

    incoming = [
        (objects, ext.at[:, :, middle, across]),
        (row_a, ext.at[:, :, beyond(row_odd), across]),
        (row_b, ext.at[:, :, beyond(1 - row_odd), across]),
        (probe, probe_in),
        (mats, mats_in),
        (amp, amp_in),
    ]
    for side, col, corner in ((1 - col_odd, col_a, corners_a), (col_odd, col_b, corners_b)):
        for rows, src in (
            (upper, corner.at[:, upper]),
            (middle, col),
            (lower, corner.at[:, pl.ds(HALO, HALO)]),
        ):
            incoming.insert(3, (src, sides.at[side, :, rows]))
    outgoing = [
        (probe_grad, probe_out),
        (sides_out.at[1 - col_odd], col_a_out),
        (sides_out.at[col_odd], col_b_out),
        (grad.at[:, :, beyond(row_odd), across], row_a_out),
        (grad.at[:, :, beyond(1 - row_odd), across], row_b_out),
        (ext.at[:, :, middle, across], center_out),
    ]
    coming = [pltpu.make_async_copy(*pair, arrive.at[i]) for i, pair in enumerate(incoming)]
    going = [pltpu.make_async_copy(*pair, leave.at[i]) for i, pair in enumerate(outgoing)]
    for copy in coming:
        copy.start()
    grad[...] = jnp.zeros_like(grad)
    for copy in coming[:-3]:
        copy.wait()
    keep = first_half((SIDE, 2 * HALO))
    for s in range(2):
        w, e = sides[0, s], sides[1, s]
        ext[s, 0, :SIDE, TILE:] = jnp.where(keep, e, pltpu.roll(w, HALO, 1))
        ext[s, 1, :SIDE, TILE:] = jnp.where(keep, pltpu.roll(e, HALO, 1), w)
    top, left = facts[0], facts[1]
    into = lax.rem(SIDE + HALO - left, SIDE)
    back = lax.rem(SIDE - HALO + left, SIDE)
    low = lax.rem(top, 8)
    rows = pl.ds(pl.multiple_of(top - low, 8), WIN + 8)

    def window(s, k):
        wide = pltpu.roll(ext[s, k, rows, :], into, 1)[:, :WIN]
        return pltpu.roll(wide, lax.rem(WIN + 8 - low, WIN + 8), 0)[:WIN]

    def place(s, k, value):
        tall = jnp.concatenate([value, jnp.zeros((8, WIN), jnp.float32)], axis=0)
        tall = pltpu.roll(tall, low, 0)
        wide = jnp.concatenate([tall, jnp.zeros((WIN + 8, SIDE - WIN), jnp.float32)], axis=1)
        grad[s, k, rows, :] = pltpu.roll(wide, back, 1)

    a_re, a_im, b_re, b_im = window(0, 0), window(0, 1), window(1, 0), window(1, 1)
    coming[-3].wait()
    p_re, p_im = probe_in[0], probe_in[1]
    u_re = p_re * a_re - p_im * a_im
    u_im = p_re * a_im + p_im * a_re
    coming[-2].wait()
    v_re, v_im = sandwich(mats_in, 0, u_re, u_im)
    e_re = v_re * b_re - v_im * b_im
    e_im = v_re * b_im + v_im * b_re
    w_re, w_im = sandwich(mats_in, 1, e_re, e_im)
    coming[-1].wait()
    size = jnp.sqrt(w_re * w_re + w_im * w_im + 1.0)
    live = jnp.where(facts[2] > 0, 2.0, 0.0)
    slope = live * (size - amp_in[...]) / size
    e_re, e_im = sandwich(mats_in, 1, slope * w_re, -slope * w_im)
    place(1, 0, -OBJ_RATE * (e_re * v_re - e_im * v_im))
    place(1, 1, OBJ_RATE * (e_re * v_im + e_im * v_re))
    v_re = e_re * b_re - e_im * b_im
    v_im = e_re * b_im + e_im * b_re
    u_re, u_im = sandwich(mats_in, 0, v_re, v_im)
    place(0, 0, -OBJ_RATE * (u_re * p_re - u_im * p_im))
    place(0, 1, OBJ_RATE * (u_re * p_im + u_im * p_re))
    probe_grad[0] = u_re * a_re - u_im * a_im
    probe_grad[1] = -(u_re * a_im + u_im * a_re)
    for s in range(2):
        real, imag = grad[s, 0, :SIDE, TILE:], grad[s, 1, :SIDE, TILE:]
        sides_out[0, s] = jnp.where(keep, pltpu.roll(real, HALO, 1), imag)
        sides_out[1, s] = jnp.where(keep, real, pltpu.roll(imag, HALO, 1))
    for copy in going[:-1]:
        copy.start()
    for s in range(2):
        for k in range(2):
            ext[s, k, middle, :TILE] = ext[s, k, middle, :TILE] + grad[s, k, middle, :TILE]
    going[-1].start()
    for copy in going:
        copy.wait()


def edge_columns(col_odd, col_a, col_b, s, start, size):
    keep = first_half((size, 2 * HALO))
    a, b = (x[s] if x.shape[1] == size else x[s, pl.ds(start, size)] for x in (col_a, col_b))
    w, e = either(col_odd, b, a), either(col_odd, a, b)
    zero = jnp.zeros_like(w)
    wr, er = pltpu.roll(w, HALO, 1), pltpu.roll(e, HALO, 1)
    return (
        (jnp.where(keep, w, zero), jnp.where(keep, zero, er)),
        (jnp.where(keep, wr, zero), jnp.where(keep, zero, e)),
    )


def relay(facts, col_a, col_b, row_a, row_b):
    row_odd = facts[3]
    for side, src in ((0, col_a), (1, col_b)):
        for s in range(2):
            upper, lower = src[s, :HALO], src[s, HALO + TILE :]
            row_a[side, s] = either(row_odd, lower, upper)
            row_b[side, s] = either(row_odd, upper, lower)


def add_sides(facts, center, col_a, col_b, row_a, row_b, tile):
    row_odd, col_odd = facts[3], facts[4]
    for s in range(2):
        edges = edge_columns(col_odd, col_a, col_b, s, HALO, TILE)
        for k in range(2):
            for half, cols in enumerate((slice(0, 128), slice(128, 256))):
                value = center[s, k, :, cols] + edges[k][half]
                a, b = row_a[s, k, :, cols], row_b[s, k, :, cols]
                tile[s, k, :HALO, cols] = value[:HALO] + either(row_odd, b, a)
                tile[s, k, HALO : TILE - HALO, cols] = value[HALO : TILE - HALO]
                tile[s, k, TILE - HALO :, cols] = value[TILE - HALO :] + either(row_odd, a, b)


def add_corners(facts, tile, relayed_a, relayed_b, new_objects):
    row_odd, col_odd = facts[3], facts[4]
    for s in range(2):
        a, b = (edge_columns(col_odd, x[0], x[1], s, 0, HALO) for x in (relayed_a, relayed_b))
        for k in range(2):
            for half, cols in enumerate((slice(0, 128), slice(128, 256))):
                first, last = a[k][half], b[k][half]
                new_objects[s, k, :HALO, cols] = tile[s, k, :HALO, cols] + either(row_odd, last, first)
                new_objects[s, k, HALO : TILE - HALO, cols] = tile[s, k, HALO : TILE - HALO, cols]
                new_objects[s, k, TILE - HALO :, cols] = tile[s, k, TILE - HALO :, cols] + either(row_odd, first, last)


def call(body, outs, *args, specs=None, scratch=(), flops=0, limit=2, name=None):
    moved = sum(math.prod(o) * 4 for o in outs)
    return pl.pallas_call(
        body,
        out_shape=[jax.ShapeDtypeStruct(o, jnp.float32) for o in outs],
        in_specs=[SMEM] + (specs or [VMEM] * (len(args) - 1)),
        out_specs=[HBM if specs else VMEM] * len(outs),
        scratch_shapes=scratch,
        compiler_params=pltpu.CompilerParams(vmem_limit_bytes=limit * MIB),
        cost_estimate=pl.CostEstimate(flops=flops, bytes_accessed=2 * moved, transcendentals=0),
        name=name,
    )(*args)


def exchanged(value, axis, first):
    pairs = [(i, i + 1) for i in range(first, lax.axis_size(axis) - 1, 2)]
    return lax.ppermute(value, axis, pairs + [(j, i) for i, j in pairs])


def swap(value, axes):
    return lax.all_to_all(value, axes, 0, 0, tiled=True)


def after(value, *others):
    return lax.optimization_barrier((value, *others))[0]


def scatter_sum(partial):
    plane = lax.axis_size(PLANE)
    core = lax.axis_index(PAIR)
    own, other = (lax.dynamic_index_in_dim(partial, k, 0, False) for k in (core, 1 - core))
    part = own + exchanged(other, PAIR, 0)
    return swap(part.reshape(plane, WIN // plane, WIN), PLANE)


def depth_sum(parts, mark):
    part = jnp.sum(after(parts, mark), axis=0)
    return swap(jnp.broadcast_to(part, (lax.axis_size(DEPTH),) + part.shape), DEPTH)


def gather_sum(parts, last):
    part = jnp.sum(parts, axis=0)
    core = lax.axis_index(PAIR)
    own = swap(jnp.broadcast_to(part, (lax.axis_size(PLANE),) + part.shape), PLANE).reshape(WIN, WIN)
    own = after(own, last)
    other = exchanged(own, PAIR, 0)
    return jnp.stack([either(core, own, other), either(core, other, own)])


def shards(objects, probe, prev_partial, offsets, counts, amplitudes):
    strip, column, corners = (2, 2, HALO, TILE), (2, TILE, 2 * HALO), (2, 2 * HALO, 2 * HALO)
    tile, strip_corners = (2, 2, TILE, TILE), (2, 2, HALO, 2 * HALO)
    whole_column = (2, SIDE, 2 * HALO)
    facts = jnp.concatenate([
        offsets.reshape(2), counts.reshape(1),
        jnp.stack([lax.axis_index("row_2"), lax.axis_index("col_1") % 2]).astype(jnp.int32),
    ])
    row_a, row_b, col_a, col_b = call(pack_sides, [strip] * 2 + [column] * 2, facts, objects, name="pack_sides")
    row_b, row_a = exchanged(row_b, ROW, 1), exchanged(row_a, ROW, 0)
    col_b, col_a = exchanged(col_b, COL, 1), exchanged(col_a, COL, 0)
    scattered = scatter_sum(prev_partial[0, 0])
    sent_a, sent_b = call(pack_corners, [corners] * 2, facts, row_a, row_b, name="pack_corners")
    corners_b, corners_a = exchanged(sent_b, COL, 1), exchanged(sent_a, COL, 0)
    deep = depth_sum(scattered, col_a)
    corners_a, deep = lax.optimization_barrier((corners_a, deep))
    center, row_a_part, row_b_part, col_a_part, col_b_part, partial = call(
        gradient,
        [tile, strip, strip, whole_column, whole_column, (2, WIN, WIN)],
        facts, objects, row_a, row_b, col_a, col_b, corners_a, corners_b, probe,
        amplitudes.reshape(WIN, WIN), jnp.asarray(operator_parts()),
        specs=[ANY] * 3 + [HBM] * 7,
        scratch=[pltpu.VMEM((2, 2, SIDE + 8, SIDE), jnp.float32)] * 2
        + [pltpu.VMEM((2, 2, SIDE, 2 * HALO), jnp.float32)] * 2
        + [pltpu.VMEM((2, WIN, WIN), jnp.float32), pltpu.VMEM((WIN, WIN), jnp.float32)]
        + [pltpu.VMEM((12, WIN, WIN), jnp.bfloat16), pltpu.VMEM((2, WIN, WIN), jnp.float32)]
        + [pltpu.SemaphoreType.DMA((12,)), pltpu.SemaphoreType.DMA((6,))],
        flops=96 * 2 * WIN**3,
        limit=60,
        name="gradient",
    )
    col_b, col_a = exchanged(col_b_part, COL, 1), exchanged(col_a_part, COL, 0)
    row_b, row_a = exchanged(row_b_part, ROW, 1), exchanged(row_a_part, ROW, 0)
    sent_a, sent_b = call(relay, [strip_corners] * 2, facts, col_a, col_b, name="relay")
    relayed_b, relayed_a = exchanged(sent_b, ROW, 1), exchanged(sent_a, ROW, 0)
    (added,) = call(add_sides, [tile], facts, center, col_a, col_b, row_a, row_b, name="add_sides")
    (new_objects,) = call(add_corners, [tile], facts, added, relayed_a, relayed_b, name="add_corners")
    rate = PROBE_RATE / math.sqrt(lax.axis_size(ROW) * lax.axis_size(COL))
    total = gather_sum(deep, partial)
    new_probe = probe - rate * total
    return (new_objects, new_probe, partial[None, None])


def solution(mesh):
    split = Mesh(mesh.devices.reshape(2, 4, 2, 4, 4), AXES)
    return jax.shard_map(
        shards,
        mesh=split,
        in_specs=(
            P(None, None, ROW, COL),
            P(),
            P(ROW, COL, None, None, None),
            P(ROW, COL, None, None),
            P(ROW, COL),
            P(ROW, COL, None, None, None),
        ),
        out_specs=(P(None, None, ROW, COL), P(), P(ROW, COL, None, None, None)),
        check_vma=False,
    )
```

```python
import math

import jax
import jax.numpy as jnp
import ml_dtypes
import numpy as np
from jax import lax
from jax.experimental import pallas as pl
from jax.experimental.pallas import tpu as pltpu
from jax.sharding import Mesh
from jax.sharding import PartitionSpec as P

WIN = 256
HALO = 64
TILE = 256
SIDE = TILE + 2 * HALO
AXES = ("row_0", "row_1", "row_2", "col_0", "col_1")
ROW = ("row_0", "row_1", "row_2")
COL = ("col_0", "col_1")
PLANE = ("row_1", "col_1")
PAIR = "row_2"
DEPTH = ("row_0", "col_0")

OBJ_RATE = 0.1
PROBE_RATE = 0.3
VMEM = pl.BlockSpec(memory_space=pltpu.VMEM)
HBM = pl.BlockSpec(memory_space=pltpu.HBM)
ANY = pl.BlockSpec(memory_space=pl.ANY)
SMEM = pl.BlockSpec(memory_space=pltpu.SMEM)
MIB = 1024 * 1024


def operator_parts():
    index = np.arange(WIN)
    angle = 2.0 * np.pi * (index[:, None] * index[None, :] % WIN) / WIN
    forward = np.exp(-1j * angle) / math.sqrt(WIN)
    freq = np.where(index < WIN // 2, index, index - WIN)
    shift = np.exp(1j * np.pi * freq.astype(np.float64) ** 2 / (4.0 * WIN))
    propagate = np.conj(forward) @ (shift[:, None] * forward)
    parts = []
    for matrix in (propagate, forward):
        matrix = (matrix + matrix.T) / 2
        halves = []
        for part in (matrix.real, matrix.imag, matrix.real + matrix.imag):
            high = part.astype(np.float32).astype(ml_dtypes.bfloat16)
            low = (part - high.astype(np.float64)).astype(np.float32)
            halves.append((high, low.astype(ml_dtypes.bfloat16)))
        parts += [high for high, _ in halves] + [low for _, low in halves]
    return np.stack(parts)


def halves_of(value):
    high = value.astype(jnp.bfloat16)
    low = (value - high.astype(jnp.float32)).astype(jnp.bfloat16)
    return high, low


def dot(left, right):
    return jnp.dot(left, right, preferred_element_type=jnp.float32)


def three(left, right):
    (left_high, left_low), (right_high, right_low) = left, right
    return dot(left_high, right_high) + (dot(left_low, right_high) + dot(left_high, right_low))


def sandwich(mats, which, real_part, imag_part):
    def halves(k):
        return mats[6 * which + k], mats[6 * which + 3 + k]

    def combine(real_real, imag_imag, both):
        return real_real - imag_imag, both - real_real - imag_imag

    parts = (real_part, imag_part, real_part + imag_part)
    real_part, imag_part = combine(*(three(halves_of(part), halves(k)) for k, part in enumerate(parts)))
    parts = (real_part, imag_part, real_part + imag_part)
    return combine(*(three(halves(k), halves_of(part)) for k, part in enumerate(parts)))


def first_half(shape):
    return lax.broadcasted_iota(jnp.int32, shape, len(shape) - 1) < HALO


def side_columns(src, s, size):
    real, imag = src[s, 0], src[s, 1]
    keep = first_half((size, 2 * HALO))
    return (
        jnp.where(keep, real[:, :128], pltpu.roll(imag[:, :128], HALO, 1)),
        jnp.where(keep, pltpu.roll(real[:, 128:], HALO, 1), imag[:, 128:]),
    )


def either(flag, when_even, when_odd):
    return jnp.where(flag == 0, when_even, when_odd)


def pack_sides(facts, objects, row_a, row_b, col_a, col_b):
    row_odd, col_odd = facts[3], facts[4]
    for s in range(2):
        top, bottom = objects[s, :, :HALO], objects[s, :, TILE - HALO :]
        row_a[s] = either(row_odd, bottom, top)
        row_b[s] = either(row_odd, top, bottom)
        first, last = side_columns(objects, s, TILE)
        col_a[s] = either(col_odd, last, first)
        col_b[s] = either(col_odd, first, last)


def pack_corners(facts, row_a, row_b, col_a, col_b):
    row_odd, col_odd = facts[3], facts[4]
    for s in range(2):
        a, b = side_columns(row_a, s, HALO), side_columns(row_b, s, HALO)
        for rows, when_even, when_odd in ((pl.ds(0, HALO), b, a), (pl.ds(HALO, HALO), a, b)):
            first, last = (either(row_odd, *pair) for pair in zip(when_even, when_odd))
            col_a[s, rows] = either(col_odd, last, first)
            col_b[s, rows] = either(col_odd, first, last)


def gradient(
    facts, objects, row_a, row_b, col_a, col_b, corners_a, corners_b, probe, amp, mats,
    center_out, row_a_out, row_b_out, col_a_out, col_b_out, probe_out,
    ext, grad, sides, sides_out, probe_in, amp_in, mats_in, probe_grad, arrive, leave,
):
    row_odd, col_odd = facts[3], facts[4]
    across = pl.ds(0, TILE)
    middle, upper, lower = pl.ds(HALO, TILE), pl.ds(0, HALO), pl.ds(HALO + TILE, HALO)

    def beyond(odd):
        return pl.ds(pl.multiple_of((1 - odd) * (HALO + TILE), HALO), HALO)

    incoming = [
        (objects, ext.at[:, :, middle, across]),
        (row_a, ext.at[:, :, beyond(row_odd), across]),
        (row_b, ext.at[:, :, beyond(1 - row_odd), across]),
        (probe, probe_in),
        (mats, mats_in),
        (amp, amp_in),
    ]
    for side, col, corner in ((1 - col_odd, col_a, corners_a), (col_odd, col_b, corners_b)):
        for rows, src in (
            (upper, corner.at[:, upper]),
            (middle, col),
            (lower, corner.at[:, pl.ds(HALO, HALO)]),
        ):
            incoming.insert(3, (src, sides.at[side, :, rows]))
    outgoing = [
        (probe_grad, probe_out),
        (sides_out.at[1 - col_odd], col_a_out),
        (sides_out.at[col_odd], col_b_out),
        (grad.at[:, :, beyond(row_odd), across], row_a_out),
        (grad.at[:, :, beyond(1 - row_odd), across], row_b_out),
        (ext.at[:, :, middle, across], center_out),
    ]
    coming = [pltpu.make_async_copy(*pair, arrive.at[i]) for i, pair in enumerate(incoming)]
    going = [pltpu.make_async_copy(*pair, leave.at[i]) for i, pair in enumerate(outgoing)]
    for copy in coming:
        copy.start()
    grad[...] = jnp.zeros_like(grad)
    for copy in coming[:-3]:
        copy.wait()
    keep = first_half((SIDE, 2 * HALO))
    for s in range(2):
        w, e = sides[0, s], sides[1, s]
        ext[s, 0, :SIDE, TILE:] = jnp.where(keep, e, pltpu.roll(w, HALO, 1))
        ext[s, 1, :SIDE, TILE:] = jnp.where(keep, pltpu.roll(e, HALO, 1), w)
    top, left = facts[0], facts[1]
    into = lax.rem(SIDE + HALO - left, SIDE)
    back = lax.rem(SIDE - HALO + left, SIDE)
    low = lax.rem(top, 8)
    rows = pl.ds(pl.multiple_of(top - low, 8), WIN + 8)

    def window(s, k):
        wide = pltpu.roll(ext[s, k, rows, :], into, 1)[:, :WIN]
        return pltpu.roll(wide, lax.rem(WIN + 8 - low, WIN + 8), 0)[:WIN]

    def place(s, k, value):
        tall = jnp.concatenate([value, jnp.zeros((8, WIN), jnp.float32)], axis=0)
        tall = pltpu.roll(tall, low, 0)
        wide = jnp.concatenate([tall, jnp.zeros((WIN + 8, SIDE - WIN), jnp.float32)], axis=1)
        grad[s, k, rows, :] = pltpu.roll(wide, back, 1)

    a_re, a_im, b_re, b_im = window(0, 0), window(0, 1), window(1, 0), window(1, 1)
    coming[-3].wait()
    p_re, p_im = probe_in[0], probe_in[1]
    u_re = p_re * a_re - p_im * a_im
    u_im = p_re * a_im + p_im * a_re
    coming[-2].wait()
    v_re, v_im = sandwich(mats_in, 0, u_re, u_im)
    e_re = v_re * b_re - v_im * b_im
    e_im = v_re * b_im + v_im * b_re
    w_re, w_im = sandwich(mats_in, 1, e_re, e_im)
    coming[-1].wait()
    size = jnp.sqrt(w_re * w_re + w_im * w_im + 1.0)
    live = jnp.where(facts[2] > 0, 2.0, 0.0)
    slope = live * (size - amp_in[...]) / size
    e_re, e_im = sandwich(mats_in, 1, slope * w_re, -slope * w_im)
    place(1, 0, -OBJ_RATE * (e_re * v_re - e_im * v_im))
    place(1, 1, OBJ_RATE * (e_re * v_im + e_im * v_re))
    v_re = e_re * b_re - e_im * b_im
    v_im = e_re * b_im + e_im * b_re
    u_re, u_im = sandwich(mats_in, 0, v_re, v_im)
    place(0, 0, -OBJ_RATE * (u_re * p_re - u_im * p_im))
    place(0, 1, OBJ_RATE * (u_re * p_im + u_im * p_re))
    probe_grad[0] = u_re * a_re - u_im * a_im
    probe_grad[1] = -(u_re * a_im + u_im * a_re)
    for s in range(2):
        real, imag = grad[s, 0, :SIDE, TILE:], grad[s, 1, :SIDE, TILE:]
        sides_out[0, s] = jnp.where(keep, pltpu.roll(real, HALO, 1), imag)
        sides_out[1, s] = jnp.where(keep, real, pltpu.roll(imag, HALO, 1))
    for copy in going[:-1]:
        copy.start()
    for s in range(2):
        for k in range(2):
            ext[s, k, middle, :TILE] = ext[s, k, middle, :TILE] + grad[s, k, middle, :TILE]
    going[-1].start()
    for copy in going:
        copy.wait()


def edge_columns(col_odd, col_a, col_b, s, start, size):
    keep = first_half((size, 2 * HALO))
    a, b = (x[s] if x.shape[1] == size else x[s, pl.ds(start, size)] for x in (col_a, col_b))
    w, e = either(col_odd, b, a), either(col_odd, a, b)
    zero = jnp.zeros_like(w)
    wr, er = pltpu.roll(w, HALO, 1), pltpu.roll(e, HALO, 1)
    return (
        (jnp.where(keep, w, zero), jnp.where(keep, zero, er)),
        (jnp.where(keep, wr, zero), jnp.where(keep, zero, e)),
    )


def relay(facts, col_a, col_b, row_a, row_b):
    row_odd = facts[3]
    for side, src in ((0, col_a), (1, col_b)):
        for s in range(2):
            upper, lower = src[s, :HALO], src[s, HALO + TILE :]
            row_a[side, s] = either(row_odd, lower, upper)
            row_b[side, s] = either(row_odd, upper, lower)


def add_sides(facts, center, col_a, col_b, row_a, row_b, tile):
    row_odd, col_odd = facts[3], facts[4]
    for s in range(2):
        edges = edge_columns(col_odd, col_a, col_b, s, HALO, TILE)
        for k in range(2):
            for half, cols in enumerate((slice(0, 128), slice(128, 256))):
                value = center[s, k, :, cols] + edges[k][half]
                a, b = row_a[s, k, :, cols], row_b[s, k, :, cols]
                tile[s, k, :HALO, cols] = value[:HALO] + either(row_odd, b, a)
                tile[s, k, HALO : TILE - HALO, cols] = value[HALO : TILE - HALO]
                tile[s, k, TILE - HALO :, cols] = value[TILE - HALO :] + either(row_odd, a, b)


def add_corners(facts, tile, relayed_a, relayed_b, new_objects):
    row_odd, col_odd = facts[3], facts[4]
    for s in range(2):
        a, b = (edge_columns(col_odd, x[0], x[1], s, 0, HALO) for x in (relayed_a, relayed_b))
        for k in range(2):
            for half, cols in enumerate((slice(0, 128), slice(128, 256))):
                first, last = a[k][half], b[k][half]
                new_objects[s, k, :HALO, cols] = tile[s, k, :HALO, cols] + either(row_odd, last, first)
                new_objects[s, k, HALO : TILE - HALO, cols] = tile[s, k, HALO : TILE - HALO, cols]
                new_objects[s, k, TILE - HALO :, cols] = tile[s, k, TILE - HALO :, cols] + either(row_odd, first, last)


def call(body, outs, *args, specs=None, scratch=(), flops=0, limit=2, name=None):
    moved = sum(math.prod(o) * 4 for o in outs)
    return pl.pallas_call(
        body,
        out_shape=[jax.ShapeDtypeStruct(o, jnp.float32) for o in outs],
        in_specs=[SMEM] + (specs or [VMEM] * (len(args) - 1)),
        out_specs=[HBM if specs else VMEM] * len(outs),
        scratch_shapes=scratch,
        compiler_params=pltpu.CompilerParams(vmem_limit_bytes=limit * MIB),
        cost_estimate=pl.CostEstimate(flops=flops, bytes_accessed=2 * moved, transcendentals=0),
        name=name,
    )(*args)


def exchanged(value, axis, first):
    pairs = [(i, i + 1) for i in range(first, lax.axis_size(axis) - 1, 2)]
    return lax.ppermute(value, axis, pairs + [(j, i) for i, j in pairs])


def swap(value, axes):
    return lax.all_to_all(value, axes, 0, 0, tiled=True)


def after(value, *others):
    return lax.optimization_barrier((value, *others))[0]


def scatter_sum(partial, mark):
    plane = lax.axis_size(PLANE)
    core = lax.axis_index(PAIR)
    own, other = (lax.dynamic_index_in_dim(partial, k, 0, False) for k in (core, 1 - core))
    part = own + exchanged(after(other, mark), PAIR, 0)
    return swap(part.reshape(plane, WIN // plane, WIN), PLANE)


def depth_sum(parts, mark):
    part = jnp.sum(after(parts, mark), axis=0)
    return swap(jnp.broadcast_to(part, (lax.axis_size(DEPTH),) + part.shape), DEPTH)


def gather_sum(parts, mark, last):
    part = jnp.sum(after(parts, mark), axis=0)
    core = lax.axis_index(PAIR)
    own = swap(jnp.broadcast_to(part, (lax.axis_size(PLANE),) + part.shape), PLANE).reshape(WIN, WIN)
    own = after(own, last)
    other = exchanged(own, PAIR, 0)
    return jnp.stack([either(core, own, other), either(core, other, own)])


def shards(objects, probe, prev_partial, offsets, counts, amplitudes):
    strip, column, corners = (2, 2, HALO, TILE), (2, TILE, 2 * HALO), (2, 2 * HALO, 2 * HALO)
    tile, strip_corners = (2, 2, TILE, TILE), (2, 2, HALO, 2 * HALO)
    whole_column = (2, SIDE, 2 * HALO)
    facts = jnp.concatenate([
        offsets.reshape(2), counts.reshape(1),
        jnp.stack([lax.axis_index("row_2"), lax.axis_index("col_1") % 2]).astype(jnp.int32),
    ])
    row_a, row_b, col_a, col_b = call(pack_sides, [strip] * 2 + [column] * 2, facts, objects, name="pack_sides")
    row_b, row_a = exchanged(row_b, ROW, 1), exchanged(row_a, ROW, 0)
    col_b, col_a = exchanged(col_b, COL, 1), exchanged(col_a, COL, 0)
    scattered = scatter_sum(prev_partial[0, 0], row_a)
    sent_a, sent_b = call(pack_corners, [corners] * 2, facts, row_a, row_b, name="pack_corners")
    corners_b, corners_a = exchanged(sent_b, COL, 1), exchanged(sent_a, COL, 0)
    deep = depth_sum(scattered, sent_a)
    corners_a, deep = lax.optimization_barrier((corners_a, deep))
    center, row_a_part, row_b_part, col_a_part, col_b_part, partial = call(
        gradient,
        [tile, strip, strip, whole_column, whole_column, (2, WIN, WIN)],
        facts, objects, row_a, row_b, col_a, col_b, corners_a, corners_b, probe,
        amplitudes.reshape(WIN, WIN), jnp.asarray(operator_parts()),
        specs=[ANY] * 3 + [HBM] * 7,
        scratch=[pltpu.VMEM((2, 2, SIDE + 8, SIDE), jnp.float32)] * 2
        + [pltpu.VMEM((2, 2, SIDE, 2 * HALO), jnp.float32)] * 2
        + [pltpu.VMEM((2, WIN, WIN), jnp.float32), pltpu.VMEM((WIN, WIN), jnp.float32)]
        + [pltpu.VMEM((12, WIN, WIN), jnp.bfloat16), pltpu.VMEM((2, WIN, WIN), jnp.float32)]
        + [pltpu.SemaphoreType.DMA((12,)), pltpu.SemaphoreType.DMA((6,))],
        flops=96 * 2 * WIN**3,
        limit=60,
        name="gradient",
    )
    col_b, col_a = exchanged(col_b_part, COL, 1), exchanged(col_a_part, COL, 0)
    row_b, row_a = exchanged(row_b_part, ROW, 1), exchanged(row_a_part, ROW, 0)
    sent_a, sent_b = call(relay, [strip_corners] * 2, facts, col_a, col_b, name="relay")
    relayed_b, relayed_a = exchanged(sent_b, ROW, 1), exchanged(sent_a, ROW, 0)
    (added,) = call(add_sides, [tile], facts, center, col_a, col_b, row_a, row_b, name="add_sides")
    (new_objects,) = call(add_corners, [tile], facts, added, relayed_a, relayed_b, name="add_corners")
    rate = PROBE_RATE / math.sqrt(lax.axis_size(ROW) * lax.axis_size(COL))
    total = gather_sum(deep, partial, new_objects)
    new_probe = probe - rate * total
    return (new_objects, new_probe, partial[None, None])


def solution(mesh):
    split = Mesh(mesh.devices.reshape(2, 4, 2, 4, 4), AXES)
    return jax.shard_map(
        shards,
        mesh=split,
        in_specs=(
            P(None, None, ROW, COL),
            P(),
            P(ROW, COL, None, None, None),
            P(ROW, COL, None, None),
            P(ROW, COL),
            P(ROW, COL, None, None, None),
        ),
        out_specs=(P(None, None, ROW, COL), P(), P(ROW, COL, None, None, None)),
        check_vma=False,
    )
```

```python
import math

import jax
import jax.numpy as jnp
import ml_dtypes
import numpy as np
from jax import lax
from jax.experimental import pallas as pl
from jax.experimental.pallas import tpu as pltpu
from jax.sharding import Mesh
from jax.sharding import PartitionSpec as P

WIN = 256
HALO = 64
TILE = 256
SIDE = TILE + 2 * HALO
AXES = ("row_0", "row_1", "row_2", "col_0", "col_1")
ROW = ("row_0", "row_1", "row_2")
COL = ("col_0", "col_1")
PLANE = ("row_1", "col_1")
PAIR = "row_2"
DEPTH = ("row_0", "col_0")

OBJ_RATE = 0.1
PROBE_RATE = 0.3
VMEM = pl.BlockSpec(memory_space=pltpu.VMEM)
HBM = pl.BlockSpec(memory_space=pltpu.HBM)
ANY = pl.BlockSpec(memory_space=pl.ANY)
SMEM = pl.BlockSpec(memory_space=pltpu.SMEM)
MIB = 1024 * 1024


def operator_parts():
    index = np.arange(WIN)
    angle = 2.0 * np.pi * (index[:, None] * index[None, :] % WIN) / WIN
    forward = np.exp(-1j * angle) / math.sqrt(WIN)
    freq = np.where(index < WIN // 2, index, index - WIN)
    shift = np.exp(1j * np.pi * freq.astype(np.float64) ** 2 / (4.0 * WIN))
    propagate = np.conj(forward) @ (shift[:, None] * forward)
    parts = []
    for matrix in (propagate, forward):
        matrix = (matrix + matrix.T) / 2
        halves = []
        for part in (matrix.real, matrix.imag, matrix.real + matrix.imag):
            high = part.astype(np.float32).astype(ml_dtypes.bfloat16)
            low = (part - high.astype(np.float64)).astype(np.float32)
            halves.append((high, low.astype(ml_dtypes.bfloat16)))
        parts += [high for high, _ in halves] + [low for _, low in halves]
    return np.stack(parts)


def halves_of(value):
    high = value.astype(jnp.bfloat16)
    low = (value - high.astype(jnp.float32)).astype(jnp.bfloat16)
    return high, low


def dot(left, right):
    return jnp.dot(left, right, preferred_element_type=jnp.float32)


def three(left, right):
    (left_high, left_low), (right_high, right_low) = left, right
    return dot(left_high, right_high) + (dot(left_low, right_high) + dot(left_high, right_low))


def sandwich(mats, which, real_part, imag_part):
    def halves(k):
        return mats[6 * which + k], mats[6 * which + 3 + k]

    def combine(real_real, imag_imag, both):
        return real_real - imag_imag, both - real_real - imag_imag

    parts = (real_part, imag_part, real_part + imag_part)
    real_part, imag_part = combine(*(three(halves_of(part), halves(k)) for k, part in enumerate(parts)))
    parts = (real_part, imag_part, real_part + imag_part)
    return combine(*(three(halves(k), halves_of(part)) for k, part in enumerate(parts)))


def first_half(shape):
    return lax.broadcasted_iota(jnp.int32, shape, len(shape) - 1) < HALO


def side_columns(src, s, size):
    real, imag = src[s, 0], src[s, 1]
    keep = first_half((size, 2 * HALO))
    return (
        jnp.where(keep, real[:, :128], pltpu.roll(imag[:, :128], HALO, 1)),
        jnp.where(keep, pltpu.roll(real[:, 128:], HALO, 1), imag[:, 128:]),
    )


def either(flag, when_even, when_odd):
    return jnp.where(flag == 0, when_even, when_odd)


def pack_sides(facts, source, row_a, row_b, col_a, col_b, objects, arrive):
    row_odd, col_odd = facts[3], facts[4]
    copies = [
        pltpu.make_async_copy(source.at[s, k], objects.at[s, k], arrive.at[s, k]) for s in range(2) for k in range(2)
    ]
    for copy in copies:
        copy.start()
    for s in range(2):
        for copy in copies[2 * s : 2 * s + 2]:
            copy.wait()
        top, bottom = objects[s, :, :HALO], objects[s, :, TILE - HALO :]
        row_a[s] = either(row_odd, bottom, top)
        row_b[s] = either(row_odd, top, bottom)
        first, last = side_columns(objects, s, TILE)
        col_a[s] = either(col_odd, last, first)
        col_b[s] = either(col_odd, first, last)


def pack_corners(facts, row_a, row_b, col_a, col_b):
    row_odd, col_odd = facts[3], facts[4]
    for s in range(2):
        a, b = side_columns(row_a, s, HALO), side_columns(row_b, s, HALO)
        for rows, when_even, when_odd in ((pl.ds(0, HALO), b, a), (pl.ds(HALO, HALO), a, b)):
            first, last = (either(row_odd, *pair) for pair in zip(when_even, when_odd))
            col_a[s, rows] = either(col_odd, last, first)
            col_b[s, rows] = either(col_odd, first, last)


def gradient(
    facts, objects, row_a, row_b, col_a, col_b, corners_a, corners_b, probe, amp, mats,
    center_out, row_a_out, row_b_out, col_a_out, col_b_out, probe_out,
    ext, grad, sides, sides_out, probe_in, amp_in, mats_in, probe_grad, arrive, leave,
):
    row_odd, col_odd = facts[3], facts[4]
    across = pl.ds(0, TILE)
    middle, upper, lower = pl.ds(HALO, TILE), pl.ds(0, HALO), pl.ds(HALO + TILE, HALO)

    def beyond(odd):
        return pl.ds(pl.multiple_of((1 - odd) * (HALO + TILE), HALO), HALO)

    incoming = [
        (objects, ext.at[:, :, middle, across]),
        (row_a, ext.at[:, :, beyond(row_odd), across]),
        (row_b, ext.at[:, :, beyond(1 - row_odd), across]),
        (probe, probe_in),
        (mats, mats_in),
        (amp, amp_in),
    ]
    for side, col, corner in ((1 - col_odd, col_a, corners_a), (col_odd, col_b, corners_b)):
        for rows, src in (
            (upper, corner.at[:, upper]),
            (middle, col),
            (lower, corner.at[:, pl.ds(HALO, HALO)]),
        ):
            incoming.insert(3, (src, sides.at[side, :, rows]))
    outgoing = [
        (probe_grad, probe_out),
        (sides_out.at[1 - col_odd], col_a_out),
        (sides_out.at[col_odd], col_b_out),
        (grad.at[:, :, beyond(row_odd), across], row_a_out),
        (grad.at[:, :, beyond(1 - row_odd), across], row_b_out),
        (ext.at[:, :, middle, across], center_out),
    ]
    coming = [pltpu.make_async_copy(*pair, arrive.at[i]) for i, pair in enumerate(incoming)]
    going = [pltpu.make_async_copy(*pair, leave.at[i]) for i, pair in enumerate(outgoing)]
    for copy in coming:
        copy.start()
    grad[...] = jnp.zeros_like(grad)
    for copy in coming[:-3]:
        copy.wait()
    keep = first_half((SIDE, 2 * HALO))
    for s in range(2):
        w, e = sides[0, s], sides[1, s]
        ext[s, 0, :SIDE, TILE:] = jnp.where(keep, e, pltpu.roll(w, HALO, 1))
        ext[s, 1, :SIDE, TILE:] = jnp.where(keep, pltpu.roll(e, HALO, 1), w)
    top, left = facts[0], facts[1]
    into = lax.rem(SIDE + HALO - left, SIDE)
    back = lax.rem(SIDE - HALO + left, SIDE)
    low = lax.rem(top, 8)
    rows = pl.ds(pl.multiple_of(top - low, 8), WIN + 8)

    def window(s, k):
        wide = pltpu.roll(ext[s, k, rows, :], into, 1)[:, :WIN]
        return pltpu.roll(wide, lax.rem(WIN + 8 - low, WIN + 8), 0)[:WIN]

    def place(s, k, value):
        tall = jnp.concatenate([value, jnp.zeros((8, WIN), jnp.float32)], axis=0)
        tall = pltpu.roll(tall, low, 0)
        wide = jnp.concatenate([tall, jnp.zeros((WIN + 8, SIDE - WIN), jnp.float32)], axis=1)
        grad[s, k, rows, :] = pltpu.roll(wide, back, 1)

    a_re, a_im, b_re, b_im = window(0, 0), window(0, 1), window(1, 0), window(1, 1)
    coming[-3].wait()
    p_re, p_im = probe_in[0], probe_in[1]
    u_re = p_re * a_re - p_im * a_im
    u_im = p_re * a_im + p_im * a_re
    coming[-2].wait()
    v_re, v_im = sandwich(mats_in, 0, u_re, u_im)
    e_re = v_re * b_re - v_im * b_im
    e_im = v_re * b_im + v_im * b_re
    w_re, w_im = sandwich(mats_in, 1, e_re, e_im)
    coming[-1].wait()
    size = jnp.sqrt(w_re * w_re + w_im * w_im + 1.0)
    live = jnp.where(facts[2] > 0, 2.0, 0.0)
    slope = live * (size - amp_in[...]) / size
    e_re, e_im = sandwich(mats_in, 1, slope * w_re, -slope * w_im)
    place(1, 0, -OBJ_RATE * (e_re * v_re - e_im * v_im))
    place(1, 1, OBJ_RATE * (e_re * v_im + e_im * v_re))
    v_re = e_re * b_re - e_im * b_im
    v_im = e_re * b_im + e_im * b_re
    u_re, u_im = sandwich(mats_in, 0, v_re, v_im)
    place(0, 0, -OBJ_RATE * (u_re * p_re - u_im * p_im))
    place(0, 1, OBJ_RATE * (u_re * p_im + u_im * p_re))
    probe_grad[0] = u_re * a_re - u_im * a_im
    probe_grad[1] = -(u_re * a_im + u_im * a_re)
    for s in range(2):
        real, imag = grad[s, 0, :SIDE, TILE:], grad[s, 1, :SIDE, TILE:]
        sides_out[0, s] = jnp.where(keep, pltpu.roll(real, HALO, 1), imag)
        sides_out[1, s] = jnp.where(keep, real, pltpu.roll(imag, HALO, 1))
    for copy in going[:-1]:
        copy.start()
    for s in range(2):
        for k in range(2):
            ext[s, k, middle, :TILE] = ext[s, k, middle, :TILE] + grad[s, k, middle, :TILE]
    going[-1].start()
    for copy in going:
        copy.wait()


def edge_columns(col_odd, col_a, col_b, s, start, size):
    keep = first_half((size, 2 * HALO))
    a, b = (x[s] if x.shape[1] == size else x[s, pl.ds(start, size)] for x in (col_a, col_b))
    w, e = either(col_odd, b, a), either(col_odd, a, b)
    zero = jnp.zeros_like(w)
    wr, er = pltpu.roll(w, HALO, 1), pltpu.roll(e, HALO, 1)
    return (
        (jnp.where(keep, w, zero), jnp.where(keep, zero, er)),
        (jnp.where(keep, wr, zero), jnp.where(keep, zero, e)),
    )


def relay(facts, col_a, col_b, row_a, row_b):
    row_odd = facts[3]
    for side, src in ((0, col_a), (1, col_b)):
        for s in range(2):
            upper, lower = src[s, :HALO], src[s, HALO + TILE :]
            row_a[side, s] = either(row_odd, lower, upper)
            row_b[side, s] = either(row_odd, upper, lower)


def add_sides(facts, center, col_a, col_b, row_a, row_b, tile):
    row_odd, col_odd = facts[3], facts[4]
    for s in range(2):
        edges = edge_columns(col_odd, col_a, col_b, s, HALO, TILE)
        for k in range(2):
            for half, cols in enumerate((slice(0, 128), slice(128, 256))):
                value = center[s, k, :, cols] + edges[k][half]
                a, b = row_a[s, k, :, cols], row_b[s, k, :, cols]
                tile[s, k, :HALO, cols] = value[:HALO] + either(row_odd, b, a)
                tile[s, k, HALO : TILE - HALO, cols] = value[HALO : TILE - HALO]
                tile[s, k, TILE - HALO :, cols] = value[TILE - HALO :] + either(row_odd, a, b)


def add_corners(facts, tile, relayed_a, relayed_b, new_objects):
    row_odd, col_odd = facts[3], facts[4]
    for s in range(2):
        a, b = (edge_columns(col_odd, x[0], x[1], s, 0, HALO) for x in (relayed_a, relayed_b))
        for k in range(2):
            for half, cols in enumerate((slice(0, 128), slice(128, 256))):
                first, last = a[k][half], b[k][half]
                new_objects[s, k, :HALO, cols] = tile[s, k, :HALO, cols] + either(row_odd, last, first)
                new_objects[s, k, HALO : TILE - HALO, cols] = tile[s, k, HALO : TILE - HALO, cols]
                new_objects[s, k, TILE - HALO :, cols] = tile[s, k, TILE - HALO :, cols] + either(row_odd, first, last)


def call(body, outs, *args, specs=None, inputs=None, scratch=(), flops=0, limit=2, name=None):
    moved = sum(math.prod(o) * 4 for o in outs)
    return pl.pallas_call(
        body,
        out_shape=[jax.ShapeDtypeStruct(o, jnp.float32) for o in outs],
        in_specs=[SMEM] + (specs or inputs or [VMEM] * (len(args) - 1)),
        out_specs=[HBM if specs else VMEM] * len(outs),
        scratch_shapes=scratch,
        compiler_params=pltpu.CompilerParams(vmem_limit_bytes=limit * MIB),
        cost_estimate=pl.CostEstimate(flops=flops, bytes_accessed=2 * moved, transcendentals=0),
        name=name,
    )(*args)


def exchanged(value, axis, first):
    pairs = [(i, i + 1) for i in range(first, lax.axis_size(axis) - 1, 2)]
    return lax.ppermute(value, axis, pairs + [(j, i) for i, j in pairs])


def swap(value, axes):
    return lax.all_to_all(value, axes, 0, 0, tiled=True)


def after(value, *others):
    return lax.optimization_barrier((value, *others))[0]


def scatter_sum(partial):
    plane = lax.axis_size(PLANE)
    core = lax.axis_index(PAIR)
    own, other = (lax.dynamic_index_in_dim(partial, k, 0, False) for k in (core, 1 - core))
    part = own + exchanged(other, PAIR, 0)
    return swap(part.reshape(plane, WIN // plane, WIN), PLANE)


def depth_sum(parts, mark):
    part = jnp.sum(after(parts, mark), axis=0)
    return swap(jnp.broadcast_to(part, (lax.axis_size(DEPTH),) + part.shape), DEPTH)


def gather_sum(parts, last):
    part = jnp.sum(parts, axis=0)
    core = lax.axis_index(PAIR)
    own = swap(jnp.broadcast_to(part, (lax.axis_size(PLANE),) + part.shape), PLANE).reshape(WIN, WIN)
    own = after(own, last)
    other = exchanged(own, PAIR, 0)
    return jnp.stack([either(core, own, other), either(core, other, own)])


def shards(objects, probe, prev_partial, offsets, counts, amplitudes):
    strip, column, corners = (2, 2, HALO, TILE), (2, TILE, 2 * HALO), (2, 2 * HALO, 2 * HALO)
    tile, strip_corners = (2, 2, TILE, TILE), (2, 2, HALO, 2 * HALO)
    whole_column = (2, SIDE, 2 * HALO)
    facts = jnp.concatenate([
        offsets.reshape(2), counts.reshape(1),
        jnp.stack([lax.axis_index("row_2"), lax.axis_index("col_1") % 2]).astype(jnp.int32),
    ])
    row_a, row_b, col_a, col_b = call(
        pack_sides,
        [strip] * 2 + [column] * 2,
        facts, objects,
        inputs=[HBM],
        scratch=[pltpu.VMEM(tile, jnp.float32), pltpu.SemaphoreType.DMA((2, 2))],
        limit=60,
        name="pack_sides",
    )
    row_b, row_a = exchanged(row_b, ROW, 1), exchanged(row_a, ROW, 0)
    col_b, col_a = exchanged(col_b, COL, 1), exchanged(col_a, COL, 0)
    scattered = scatter_sum(prev_partial[0, 0])
    sent_a, sent_b = call(pack_corners, [corners] * 2, facts, row_a, row_b, name="pack_corners")
    corners_b, corners_a = exchanged(sent_b, COL, 1), exchanged(sent_a, COL, 0)
    deep = depth_sum(scattered, col_a)
    corners_a, deep = lax.optimization_barrier((corners_a, deep))
    center, row_a_part, row_b_part, col_a_part, col_b_part, partial = call(
        gradient,
        [tile, strip, strip, whole_column, whole_column, (2, WIN, WIN)],
        facts, objects, row_a, row_b, col_a, col_b, corners_a, corners_b, probe,
        amplitudes.reshape(WIN, WIN), jnp.asarray(operator_parts()),
        specs=[ANY] * 3 + [HBM] * 7,
        scratch=[pltpu.VMEM((2, 2, SIDE + 8, SIDE), jnp.float32)] * 2
        + [pltpu.VMEM((2, 2, SIDE, 2 * HALO), jnp.float32)] * 2
        + [pltpu.VMEM((2, WIN, WIN), jnp.float32), pltpu.VMEM((WIN, WIN), jnp.float32)]
        + [pltpu.VMEM((12, WIN, WIN), jnp.bfloat16), pltpu.VMEM((2, WIN, WIN), jnp.float32)]
        + [pltpu.SemaphoreType.DMA((12,)), pltpu.SemaphoreType.DMA((6,))],
        flops=96 * 2 * WIN**3,
        limit=60,
        name="gradient",
    )
    col_b, col_a = exchanged(col_b_part, COL, 1), exchanged(col_a_part, COL, 0)
    row_b, row_a = exchanged(row_b_part, ROW, 1), exchanged(row_a_part, ROW, 0)
    sent_a, sent_b = call(relay, [strip_corners] * 2, facts, col_a, col_b, name="relay")
    relayed_b, relayed_a = exchanged(sent_b, ROW, 1), exchanged(sent_a, ROW, 0)
    (added,) = call(add_sides, [tile], facts, center, col_a, col_b, row_a, row_b, name="add_sides")
    (new_objects,) = call(add_corners, [tile], facts, added, relayed_a, relayed_b, name="add_corners")
    rate = PROBE_RATE / math.sqrt(lax.axis_size(ROW) * lax.axis_size(COL))
    total = gather_sum(deep, partial)
    new_probe = probe - rate * total
    return (new_objects, new_probe, partial[None, None])


def solution(mesh):
    split = Mesh(mesh.devices.reshape(2, 4, 2, 4, 4), AXES)
    return jax.shard_map(
        shards,
        mesh=split,
        in_specs=(
            P(None, None, ROW, COL),
            P(),
            P(ROW, COL, None, None, None),
            P(ROW, COL, None, None),
            P(ROW, COL),
            P(ROW, COL, None, None, None),
        ),
        out_specs=(P(None, None, ROW, COL), P(), P(ROW, COL, None, None, None)),
        check_vma=False,
    )
```
